128 devices in a mesh: row: 16 (over x, z_hi, core), col: 8 (over z_lo, y).
Axes of the slice: x: 4, y: 4, z: 4 (z_hi: 2, z_lo: 2; z = z_hi * 2 + z_lo), core: 2. Of those that a mesh axis runs over, the one named last changes fastest.
Arguments:
- source_vectors: float32 [1024, 73728], P(('row', 'col')), may hold values from -6 to 6
- source_slot: int32 [1024], P('col'), may hold values from 0 to 1023, as said below
- reflectors: float32 [73728, 1024], P('row'), may hold values from -6 to 6
- panel_offsets: int32 [16], replicated, may hold values from 0 to 18432
Outputs:
- vectors: float32 [1024, 73728], P('col', 'row')
The draws below stay inside these ranges and needn't reach their ends.
Inputs may be any that keep to these rules, and one draw needn't show every extreme that they name: `source_slot`: A permutation of 0 .. 1023; for each c, the entries c * 128 .. (c + 1) * 128 - 1 are exactly the values s with (s // 8) % 8 == c.
All inputs are finite; a program needn't handle non-finite values.
Results may differ from the reference program's by a relative error of at most 0.0003.
Values sent between devices are 32-bit elements; how exact they have to be, the bound alone decides.
No kernel may reach another device: no remote copies, remote signals or barrier semaphores. Data moves between devices by JAX's collectives and lax.ppermute only.
A program may use at most 128 MiB of HBM per device.

```python
import jax
import jax.numpy as jnp
from jax import lax

K = 1024
NB = 64
PANELS = 16
NUM_ROWS = 73728
SRC_BLOCK = 8
COL_BLOCK = 128
COL_GROUPS = 8


def draw_source_slot(key, part):
    key = jax.random.fold_in(key, 7)
    within = jnp.arange(COL_BLOCK, dtype=jnp.int32)[None, :]
    groups = jnp.arange(COL_GROUPS, dtype=jnp.int32)[:, None]
    base = (within // SRC_BLOCK * COL_GROUPS + groups) * SRC_BLOCK + within % SRC_BLOCK
    mixed_order = jax.random.permutation(key, base, axis=1, independent=True)
    return mixed_order.reshape(-1).astype(jnp.int32)


def set_ends(entries, stream_key, low, high):
    longest = entries.shape.index(max(entries.shape))
    spots = []
    for shift in (0, 1):
        where = [jax.random.randint(jax.random.fold_in(stream_key, axis), (), 0, length) for axis, length in enumerate(entries.shape)]
        where[longest] = (where[longest] + shift) % entries.shape[longest]
        spots.append(tuple(where))
    return entries.at[spots[0]].set(low).at[spots[1]].set(high)


def levels(stream_key, shape, pieces, low, largest):
    def one(axis_at, parts):
        heights = jax.random.uniform(jax.random.fold_in(jax.random.fold_in(stream_key, 6), axis_at), (parts,), jnp.float32, low / len(pieces), largest / len(pieces))
        return jnp.repeat(jnp.exp(heights), shape[axis_at] // parts).reshape((-1,) + (1,) * (len(shape) - axis_at - 1))

    factor_of = one(*pieces[0])
    for cut in pieces[1:]:
        factor_of = factor_of * one(*cut)
    return factor_of


def scatter_about(stream_key, dims, spread, most, pieces=(), kind=jnp.bfloat16):
    gain = levels(stream_key, dims, pieces, -0.22, 0.18) if pieces else 1.0
    drawn = jax.random.normal(stream_key, dims, jnp.float32) * spread * gain
    return jnp.minimum(jnp.maximum(drawn, -most), most).astype(kind)


def setup_inputs(seed: int = 0) -> dict:
    splits = jax.random.split(jax.random.key(seed), 5)
    return {
        "source_vectors": scatter_about(splits[0], (K, NUM_ROWS), 1.0, 6.0, ((0, 128),), jnp.float32),
        "source_slot": draw_source_slot(jax.random.fold_in(splits[4], 71), 0),
        "reflectors": scatter_about(splits[2], (NUM_ROWS, PANELS * NB), 1.0, 6.0, ((0, 16),), jnp.float32),
        "panel_offsets": set_ends(jax.random.randint(splits[3], (PANELS,), 0, NUM_ROWS // 4 + 1), jax.random.fold_in(splits[3], 1), 0, (NUM_ROWS // 4 + 1) - 1).astype(jnp.int32),
    }


def reflector_block(reflectors, panel_offsets, row_start, width):
    count = reflectors.shape[0]
    total = reflectors.shape[1]
    panels = panel_offsets.shape[0]
    rows = row_start + jnp.arange(count, dtype=jnp.int32)[:, None]
    columns = jnp.arange(total, dtype=jnp.int32)
    owner = jnp.arange(panels, dtype=jnp.int32)[:, None] == (columns // width)[None, :]
    lead = jnp.sum(jnp.where(owner, panel_offsets[:, None], 0), axis=0).astype(jnp.int32) + columns % width
    lead = lead[None, :]
    return jnp.where(rows < lead, 0.0, jnp.where(rows == lead, 1.0, reflectors)).astype(jnp.float32)


def invert_upper(blocks):
    width = blocks.shape[-1]
    half = jnp.diagonal(blocks, axis1=1, axis2=2) / 2.0
    strict = jnp.triu(blocks, 1)
    power = -strict / half[:, :, None]
    identity = jnp.eye(width, dtype=blocks.dtype)[None, :, :]
    inverse = identity + power
    for level in range(max(1, (width - 1).bit_length()) - 1):
        power = jnp.einsum("nab,nbc->nac", power, power, precision=lax.Precision.HIGHEST)
        inverse = jnp.einsum("nab,nbc->nac", inverse, identity + power, precision=lax.Precision.HIGHEST)
    return inverse / half[:, None, :]


def apply_panel(vectors, summed, panel, factor):
    weighted = jnp.dot(summed, factor.T, precision=lax.Precision.HIGHEST)
    change = lax.dot_general(weighted, panel, (((1,), (1,)), ((), ())), precision=lax.Precision.HIGHEST)
    return vectors - change


def reference(source_vectors, source_slot, reflectors, panel_offsets):
    panels = panel_offsets.shape[0]
    width = reflectors.shape[1] // panels
    reflect = reflector_block(reflectors, panel_offsets, 0, width)
    shaped = reflect.reshape(reflect.shape[0], panels, width)
    grams = jnp.einsum("rpa,rpb->pab", shaped, shaped, precision=lax.Precision.HIGHEST)
    factors = invert_upper(grams)
    vectors = jnp.take(source_vectors, source_slot, axis=0)
    for index in reversed(range(panels)):
        panel = reflect[:, index * width:(index + 1) * width]
        summed = jnp.dot(vectors, panel, precision=lax.Precision.HIGHEST)
        vectors = apply_panel(vectors, summed, panel, factors[index])
    return vectors
```

```python
import functools

import jax
import jax.numpy as jnp
from jax import lax
from jax.experimental import pallas as pl
from jax.experimental.pallas import tpu as pltpu
from jax.sharding import PartitionSpec as P

F32 = jnp.float32
BF16 = jnp.bfloat16
TILE = 512
BLOCK = 128


def halves(x):
    high = x.astype(BF16)
    return high, (x - high.astype(F32)).astype(BF16)


def dot(a, b, ca=1, cb=0):
    return lax.dot_general(a, b, (((ca,), (cb,)), ((), ())), preferred_element_type=F32)


def dot3(a, b, ca=1, cb=0):
    ah, al = halves(a)
    bh, bl = halves(b)
    return dot(ah, bh, ca, cb) + (dot(ah, bl, ca, cb) + dot(al, bh, ca, cb))


def basis_halves(tile_ref, lead_ref, first_row):
    x = tile_ref[...]
    rows = first_row + lax.broadcasted_iota(jnp.int32, x.shape, 0)
    lead = lead_ref[...]
    return halves(jnp.where(rows < lead, 0.0, jnp.where(rows == lead, 1.0, x)))


def gram_kernel(place_ref, lead_ref, tile_ref, out_ref, high_ref, low_ref):
    step = pl.program_id(0)
    tile = tile_ref.shape[0]
    high, low = basis_halves(tile_ref, lead_ref, place_ref[0] + step * tile)
    high_ref[...] = high
    low_ref[...] = low
    mine = pl.ds(pl.multiple_of(place_ref[1] * BLOCK, BLOCK), BLOCK)
    left = jnp.concatenate([high_ref[:, mine], low_ref[:, mine]], axis=1)
    both = dot(left, high, 0, 0)
    total = both[:BLOCK] + (both[BLOCK:] + dot(left[:, :BLOCK], low, 0, 0))

    @pl.when(step == 0)
    def _():
        out_ref[...] = total

    @pl.when(step > 0)
    def _():
        out_ref[...] += total


def product_kernel(place_ref, lead_ref, vec_ref, tile_ref, out_ref):
    step = pl.program_id(0)
    tile = tile_ref.shape[0]
    high, low = basis_halves(tile_ref, lead_ref, place_ref[0] + step * tile)
    vh, vl = halves(vec_ref[...])
    count = vh.shape[0]
    both = dot(jnp.concatenate([vh, vl], axis=0), high)
    total = both[:count] + (both[count:] + dot(vh, low))

    @pl.when(step == 0)
    def _():
        out_ref[...] = total

    @pl.when(step > 0)
    def _():
        out_ref[...] += total


def inverse_kernel(gram_ref, out_ref, low_ref):
    total = out_ref.shape[0]
    blocks = total // BLOCK
    r = lax.broadcasted_iota(jnp.int32, (BLOCK, BLOCK), 0)
    c = lax.broadcasted_iota(jnp.int32, (BLOCK, BLOCK), 1)
    for q in range(blocks):
        low_ref[q * BLOCK : (q + 1) * BLOCK, :] = gram_ref[:, q].reshape(BLOCK, total)
    out_ref[...] = jnp.zeros_like(out_ref)
    lows, inverses = [], []
    for q in range(blocks):
        part = pl.ds(q * BLOCK, BLOCK)
        square = low_ref[part, part]
        lows.append(square)
        inverses.append(jnp.where(r == c, 2.0 / square, 0.0))
    size = 1
    while size < BLOCK:
        pair = (r // (2 * size) == c // (2 * size)) & (r // size > c // size)
        mids = [dot3(jnp.where(pair, lows[q], 0.0), inverses[q]) for q in range(blocks)]
        inverses = [inverses[q] - dot3(inverses[q], mids[q]) for q in range(blocks)]
        size *= 2
    for q in range(blocks):
        part = pl.ds(q * BLOCK, BLOCK)
        out_ref[part, part] = inverses[q]
    while size < total:
        for start in range(0, total, 2 * size):
            a, b = pl.ds(start, size), pl.ds(start + size, size)
            mid = dot3(low_ref[b, a], out_ref[a, a])
            out_ref[b, a] = -dot3(out_ref[b, b], mid)
        size *= 2


def change_kernel(
    place_ref, lead_ref, order_ref, summed_ref, inverse_ref, vec_ref, tile_ref, out_ref, wh_ref, wl_ref
):
    step = pl.program_id(0)
    tile = tile_ref.shape[0]
    count = vec_ref.shape[0]

    @pl.when(step == 0)
    def _():
        wh, wl = halves(dot3(summed_ref[...], inverse_ref[...]))
        wh_ref[...] = wh
        wl_ref[...] = wl

    high, low = basis_halves(tile_ref, lead_ref, place_ref[0] + step * tile)
    wh = wh_ref[...]
    both = dot(jnp.concatenate([wh, wl_ref[...]], axis=0), high, 1, 1)
    value = vec_ref[...] - (both[:count] + (both[count:] + dot(wh, low, 1, 1)))
    v1 = value.astype(BF16)
    rest = value - v1.astype(F32)
    v2 = rest.astype(BF16)
    v3 = (rest - v2.astype(F32)).astype(BF16)
    order = order_ref[...]
    out_ref[...] = dot(order, v1) + (dot(order, v2) + dot(order, v3))


def params(mib):
    return pltpu.CompilerParams(vmem_limit_bytes=mib << 20)


def per_device(source_vectors, source_slot, reflectors, panel_offsets):
    row_count = lax.axis_size("row")
    col_count = lax.axis_size("col")
    src_block = source_vectors.shape[0]
    rows_dev, total = reflectors.shape
    width = total // panel_offsets.shape[0]
    count = src_block * row_count
    steps = rows_dev // TILE

    place = jnp.stack([lax.axis_index("row") * rows_dev, lax.axis_index("col")]).astype(jnp.int32)
    lead = (panel_offsets[:, None] + jnp.arange(width, dtype=jnp.int32)[None, :]).reshape(1, total)
    placing = source_slot // (col_count * src_block) * src_block + source_slot % src_block
    order = (placing[:, None] == jnp.arange(count, dtype=jnp.int32)[None, :]).astype(BF16)

    smem = pl.BlockSpec(memory_space=pltpu.SMEM)
    lead_spec = pl.BlockSpec((1, total), lambda i: (0, 0))
    tile_spec = pl.BlockSpec((TILE, total), lambda i: (i, 0))
    vec_spec = pl.BlockSpec((count, TILE), lambda i: (0, i))

    def whole(shape):
        return pl.BlockSpec(shape, lambda i: tuple(0 for _ in shape))

    shaped = source_vectors.reshape(src_block, row_count, rows_dev).transpose(1, 0, 2)
    received = lax.all_to_all(shaped, "row", 0, 0, tiled=True).reshape(count, rows_dev)

    gram = pl.pallas_call(
        gram_kernel,
        grid=(steps,),
        in_specs=[smem, lead_spec, tile_spec],
        out_specs=whole((BLOCK, total)),
        out_shape=jax.ShapeDtypeStruct((BLOCK, total), F32),
        scratch_shapes=[pltpu.VMEM((TILE, total), BF16), pltpu.VMEM((TILE, total), BF16)],
        compiler_params=params(24),
        cost_estimate=pl.CostEstimate(
            flops=6 * rows_dev * BLOCK * total, bytes_accessed=4 * rows_dev * total, transcendentals=0
        ),
        name="gram",
    )(place, lead, reflectors)
    pieces = lax.all_to_all(gram.reshape(row_count, BLOCK // row_count, total), "row", 0, 0, tiled=True)
    piece = jnp.sum(pieces, axis=0)
    everyone = row_count * col_count
    spread = jnp.broadcast_to(piece[None], (everyone,) + piece.shape)
    grams = lax.all_to_all(spread, ("row", "col"), 0, 0, tiled=True)
    grams = grams.reshape(row_count, col_count, BLOCK // row_count, total)
    inverse = pl.pallas_call(
        inverse_kernel,
        out_shape=jax.ShapeDtypeStruct((total, total), F32),
        scratch_shapes=[pltpu.VMEM((total, total), F32)],
        compiler_params=params(32),
        cost_estimate=pl.CostEstimate(flops=2 * total**3, bytes_accessed=8 * total**2, transcendentals=0),
        name="inverse",
    )(grams)

    partial_value = pl.pallas_call(
        product_kernel,
        grid=(steps,),
        in_specs=[smem, lead_spec, vec_spec, tile_spec],
        out_specs=whole((count, total)),
        out_shape=jax.ShapeDtypeStruct((count, total), F32),
        compiler_params=params(24),
        cost_estimate=pl.CostEstimate(
            flops=6 * rows_dev * count * total, bytes_accessed=4 * rows_dev * (total + count), transcendentals=0
        ),
        name="product",
    )(place, lead, received, reflectors)
    parts = lax.all_to_all(partial_value.reshape(row_count, src_block, total), "row", 0, 0, tiled=True)
    mine = jnp.sum(parts, axis=0)
    spread = jnp.broadcast_to(mine[None], (row_count,) + mine.shape)
    summed = lax.all_to_all(spread, "row", 0, 0, tiled=True).reshape(count, total)

    return pl.pallas_call(
        change_kernel,
        grid=(steps,),
        in_specs=[smem, lead_spec, whole((count, count)), whole((count, total)), whole((total, total)), vec_spec, tile_spec],
        out_specs=vec_spec,
        out_shape=jax.ShapeDtypeStruct((count, rows_dev), F32),
        scratch_shapes=[pltpu.VMEM((count, total), BF16), pltpu.VMEM((count, total), BF16)],
        compiler_params=params(32),
        cost_estimate=pl.CostEstimate(
            flops=6 * rows_dev * count * total, bytes_accessed=4 * rows_dev * (total + 2 * count), transcendentals=0
        ),
        name="change",
    )(place, lead, order, summed, inverse, received, reflectors)


def solution(mesh):
    in_specs = (P(("row", "col"), None), P("col"), P("row", None), P())
    out_specs = P("col", "row")
    return jax.shard_map(per_device, mesh=mesh, in_specs=in_specs, out_specs=out_specs, check_vma=False)
```

```python
import jax
import jax.numpy as jnp
from jax import lax
from jax.experimental import pallas as pl
from jax.experimental.pallas import tpu as pltpu
from jax.sharding import PartitionSpec as P

F32 = jnp.float32
BF16 = jnp.bfloat16
TILE = 256
CHUNK = 16
SLOTS = 4
BLOCK = 128
HALF = 64
CORE, Z_HIGH, Z_LOW = 8, 16, 4
X_STEPS = (32, 96, 64)
Y_STEPS = (1, 3, 2)


def halves(x):
    high = x.astype(BF16)
    return high, (x - high.astype(F32)).astype(BF16)


def dot(a, b, ca=1, cb=0):
    return lax.dot_general(a, b, (((ca,), (cb,)), ((), ())), preferred_element_type=F32)


def dot3(a, b):
    ah, al = halves(a)
    bh, bl = halves(b)
    return dot(ah, bh) + (dot(ah, bl) + dot(al, bh))


def span(start, size):
    return pl.ds(start if isinstance(start, int) else pl.multiple_of(start, size), size)


def sweep(first, lead_ref, tiles_ref, slot_ref, even_ref, odd_ref, sem, use, keep=None):
    steps = tiles_ref.shape[0] // TILE
    total = tiles_ref.shape[1]
    index = lax.broadcasted_iota(jnp.int32, (CHUNK, total), 0)

    def fetch(step):
        slot = step % SLOTS if isinstance(step, int) else lax.rem(step, SLOTS)
        return pltpu.make_async_copy(tiles_ref.at[span(step * TILE, TILE), :], slot_ref.at[slot], sem.at[slot])

    def halve(step, ref):
        slot = step % SLOTS if isinstance(step, int) else lax.rem(step, SLOTS)
        start = lead_ref[...] - (first + step * TILE)
        for at in range(0, TILE, CHUNK):
            x = slot_ref[slot, at : at + CHUNK, :]
            lead = start - at
            x = jnp.where(index < lead, 0.0, jnp.where(index == lead, 1.0, x))
            high, low = halves(x)
            ref[0, at : at + CHUNK, :] = high
            ref[1, at : at + CHUNK, :] = low
            if keep is not None:
                part = span(step * TILE + at, CHUNK)
                keep[0][part, :] = high
                keep[1][part, :] = low

    for step in range(SLOTS - 1):
        fetch(step).start()
    fetch(0).wait()
    halve(0, even_ref)

    @pl.loop(0, steps // 2 - 1)
    def _(pair):
        for step, now, later in ((2 * pair, even_ref, odd_ref), (2 * pair + 1, odd_ref, even_ref)):

            @pl.when(step + SLOTS - 1 < steps)
            def _():
                fetch(step + SLOTS - 1).start()

            fetch(step + 1).wait()
            use(step, now)
            halve(step + 1, later)

    fetch(steps - 1).wait()
    use(steps - 2, even_ref)
    halve(steps - 1, odd_ref)
    use(steps - 1, odd_ref)


def gram_kernel(place_ref, lead_ref, tiles_ref, keep_ref, send_ref, slot_ref, even_ref, odd_ref, sum_ref, pack_ref, sem):
    total = tiles_ref.shape[1]
    first, core, x_at, col = place_ref[0], place_ref[1], place_ref[2], place_ref[3]
    parity = lax.rem(col, 2)
    block_a, block_b = col // 2, (15 - col) // 2
    lane_half = lax.broadcasted_iota(jnp.int32, (1, BLOCK), 1) // HALF
    from_a = jnp.where(lane_half == parity, 1.0, 0.0).astype(BF16)
    from_b = jnp.where(lane_half == parity, 0.0, 1.0).astype(BF16)

    def use(step, ref):
        def chosen(which):
            a = ref[which, :, span(block_a * BLOCK, BLOCK)]
            b = ref[which, :, span(block_b * BLOCK, BLOCK)]
            return a * from_a + b * from_b

        left = jnp.concatenate([chosen(0), chosen(1)], axis=1).T
        both = dot(left, ref[0])
        sum_ref[...] += both[:BLOCK] + (both[BLOCK:] + dot(left[:BLOCK], ref[1]))

    sum_ref[...] = jnp.zeros_like(sum_ref)
    sweep(first, lead_ref, tiles_ref, slot_ref, even_ref, odd_ref, sem, use)

    blocks_b = block_b + 1
    pack_ref[:, :total] = sum_ref[span((1 - parity) * HALF, HALF), :]
    for m in range(4):

        @pl.when(m <= block_a)
        def _():
            pack_ref[:, span((blocks_b + m) * BLOCK, BLOCK)] = sum_ref[
                span(parity * HALF, HALF), m * BLOCK : (m + 1) * BLOCK
            ]

    for k in range(4):
        at = jnp.bitwise_xor(x_at, k) * 8
        keep_ref[k * 8 : k * 8 + 8, :] = pack_ref[span(core * 32 + at, 8), :]
        send_ref[k * 8 : k * 8 + 8, :] = pack_ref[span((1 - core) * 32 + at, 8), :]


def product_kernel(
    place_ref, lead_ref, vec_ref, tiles_ref, high_ref, low_ref, keep_ref, send_ref, slot_ref, even_ref, odd_ref, sum_ref, sem
):
    count = vec_ref.shape[0]
    core, x_at = place_ref[1], place_ref[2]

    def use(step, ref):
        vh, vl = halves(vec_ref[:, span(step * TILE, TILE)])
        both = dot(jnp.concatenate([vh, vl], axis=0), ref[0])
        sum_ref[...] += both[:count] + (both[count:] + dot(vh, ref[1]))

    sum_ref[...] = jnp.zeros_like(sum_ref)
    sweep(place_ref[0], lead_ref, tiles_ref, slot_ref, even_ref, odd_ref, sem, use, (high_ref, low_ref))
    for k in range(4):
        at = jnp.bitwise_xor(x_at, k) * 16
        keep_ref[k * 16 : k * 16 + 16, :] = sum_ref[span(core * 64 + at, 16), :]
        send_ref[k * 16 : k * 16 + 16, :] = sum_ref[span((1 - core) * 64 + at, 16), :]


def join_kernel(*refs):
    *parts, out_ref = refs
    at = 0
    for part in parts:
        if part.ndim == 3:
            out_ref[at : at + part.shape[0]] = part[...]
            at += part.shape[0]


def reorder_kernel(order_ref, vec_ref, out_ref):
    order = order_ref[...]

    @pl.loop(0, vec_ref.shape[1] // TILE)
    def _(step):
        part = span(step * TILE, TILE)
        value = vec_ref[:, part]
        v1 = value.astype(BF16)
        rest = value - v1.astype(F32)
        v2, v3 = halves(rest)
        out_ref[:, part] = dot(order, v1) + (dot(order, v2) + dot(order, v3))


def inverse_kernel(place_ref, *refs):
    *gram_refs, high_ref, low_ref, lower_ref, out_ref = refs
    total = out_ref.shape[0]
    blocks = total // BLOCK
    core, x_at, col = place_ref[1], place_ref[2], place_ref[3]
    r = lax.broadcasted_iota(jnp.int32, (BLOCK, BLOCK), 0)
    c = lax.broadcasted_iota(jnp.int32, (BLOCK, BLOCK), 1)
    for q in range(8):
        width = (q // 2 + 1) * BLOCK
        rest = 9 * BLOCK - width
        away = jnp.bitwise_xor(col, q)
        for k in range(8):
            mine = lax.rem(away, 4) * 2 + away // 4
            near = jnp.bitwise_xor(x_at, k % 4)
            for j, ref in enumerate(gram_refs):

                @pl.when((near == j % 4) & (jnp.bitwise_xor(core, k // 4) == j // 4))
                def _():
                    piece = ref[mine]
                    top, low = (15 - q) * HALF + k * 8, q * HALF + k * 8
                    lower_ref[top : top + 8, :rest] = piece[:, :rest]
                    lower_ref[low : low + 8, :width] = piece[:, rest:]

    out_ref[...] = jnp.zeros_like(out_ref)
    lows, inverses = [], []
    for q in range(blocks):
        part = pl.ds(q * BLOCK, BLOCK)
        square = lower_ref[part, part]
        lows.append(square)
        inverses.append(jnp.where(r == c, 2.0 / square, 0.0))
    same = r // HALF == c // HALF
    scales = [jnp.sum(inverses[q], axis=0, keepdims=True) for q in range(blocks)]
    scaled = [jnp.sum(inverses[q], axis=1, keepdims=True) for q in range(blocks)]
    powers = [jnp.where(same & (r > c), -lows[q] * scaled[q], 0.0) for q in range(blocks)]
    identity = jnp.where(r == c, 1.0, 0.0)
    products = [identity + powers[q] for q in range(blocks)]
    for _ in range(5):
        powers = [dot3(powers[q], powers[q]) for q in range(blocks)]
        products = [products[q] + dot3(products[q], powers[q]) for q in range(blocks)]
    inverses = [products[q] * scales[q] for q in range(blocks)]
    pair = (r >= HALF) & (c < HALF)
    mids = [dot3(jnp.where(pair, lows[q], 0.0), inverses[q]) for q in range(blocks)]
    inverses = [inverses[q] - dot3(inverses[q], mids[q]) for q in range(blocks)]
    size = BLOCK
    for q in range(blocks):
        part = pl.ds(q * BLOCK, BLOCK)
        out_ref[part, part] = inverses[q]
    while size < total:
        for start in range(0, total, 2 * size):
            a, b = pl.ds(start, size), pl.ds(start + size, size)
            mid = dot3(lower_ref[b, a], out_ref[a, a])
            out_ref[b, a] = -dot3(out_ref[b, b], mid)
        size *= 2
    high, low = halves(out_ref[...])
    high_ref[...] = high
    low_ref[...] = low


def change_kernel(place_ref, order_ref, *refs):
    *sum_refs, th_ref, tl_ref, vec_ref, high_ref, low_ref, out_ref, sum_ref, w_ref, put_ref, put_sem = refs
    count, rows = vec_ref.shape
    steps = rows // TILE
    core, x_at = place_ref[1], place_ref[2]
    for j, ref in enumerate(sum_refs):
        at = jnp.bitwise_xor(core, j // 4) * 64 + jnp.bitwise_xor(x_at, j % 4) * 16
        sum_ref[span(at, 16), :] = ref[...]
    yh, yl = halves(sum_ref[...])
    both = dot(jnp.concatenate([yh, yl], axis=0), th_ref[...])
    weighted = both[:count] + (both[count:] + dot(yh, tl_ref[...]))
    order = order_ref[...]
    wh, wl = halves(weighted)
    w_ref[:count, :] = dot(order, wh).astype(BF16)
    w_ref[count:, :] = dot(order, wl).astype(BF16)

    def put(step, slot):
        return pltpu.make_async_copy(put_ref.at[slot], out_ref.at[:, span(step * TILE, TILE)], put_sem.at[slot])

    @pl.loop(0, steps)
    def _(step):
        at = lax.rem(step, 2)
        part = span(step * TILE, TILE)
        both = dot(w_ref[...], high_ref[part, :], 1, 1)
        change = both[:count] + (both[count:] + dot(w_ref[:count, :], low_ref[part, :], 1, 1))

        @pl.when(step >= 2)
        def _():
            put(step - 2, at).wait()

        put_ref[at] = vec_ref[:, part] - change
        put(step, at).start()

    for step in range(max(0, steps - 2), steps):
        put(step, step % 2).wait()


def params(mib):
    return pltpu.CompilerParams(vmem_limit_bytes=mib << 20)


def cost(flops, moved):
    return pl.CostEstimate(flops=flops, bytes_accessed=moved, transcendentals=0)


def swap(x, bits):
    return lax.ppermute(x, ("row", "col"), [(i, i ^ bits) for i in range(128)])


def scattered_sum(keep, send, size):
    both = keep + swap(send, CORE)
    total = both[:size]
    for k, bits in ((1, 32), (3, 96), (2, 64)):
        total = total + swap(both[k * size : (k + 1) * size], bits)
    return total + swap(total, Z_HIGH)


def gather(x, steps):
    near, far, across = (swap(x, bits) for bits in steps)
    return [x, near, across, far]


def join(*parts):
    places = [pl.BlockSpec(memory_space=pltpu.VMEM if part.ndim == 3 else pl.ANY) for part in parts]
    deep = sum(part.shape[0] for part in parts if part.ndim == 3)
    return pl.pallas_call(
        join_kernel,
        in_specs=places,
        out_specs=pl.BlockSpec(memory_space=pltpu.VMEM),
        out_shape=jax.ShapeDtypeStruct((deep,) + parts[-1].shape[1:], F32),
        compiler_params=params(4),
        cost_estimate=cost(1 << 16, 1 << 16),
        name="join",
    )(*parts)


def per_device(source_vectors, source_slot, reflectors, panel_offsets):
    row_count = lax.axis_size("row")
    col_count = lax.axis_size("col")
    src_block = source_vectors.shape[0]
    rows_dev, total = reflectors.shape
    width = total // panel_offsets.shape[0]
    count = src_block * row_count

    row = lax.axis_index("row")
    place = jnp.stack([row * rows_dev, row % 2, row // 4, lax.axis_index("col")]).astype(jnp.int32)
    lead = (panel_offsets[:, None] + jnp.arange(width, dtype=jnp.int32)[None, :]).reshape(1, total)
    placing = source_slot // (col_count * src_block) * src_block + source_slot % src_block
    order = (placing[:, None] == jnp.arange(count, dtype=jnp.int32)[None, :]).astype(BF16)

    smem = pl.BlockSpec(memory_space=pltpu.SMEM)
    vmem = pl.BlockSpec(memory_space=pltpu.VMEM)
    hbm = pl.BlockSpec(memory_space=pltpu.HBM)
    held = pltpu.VMEM((rows_dev, total), BF16)

    shaped = source_vectors.reshape(src_block, row_count, rows_dev).transpose(1, 0, 2)
    received = lax.all_to_all(shaped, "row", 0, 0, tiled=True).reshape(count, rows_dev)

    packed = 9 * BLOCK
    swept = [
        pltpu.VMEM((SLOTS, TILE, total), F32),
        pltpu.VMEM((2, TILE, total), BF16),
        pltpu.VMEM((2, TILE, total), BF16),
        pltpu.VMEM((BLOCK, total), F32),
    ]
    near_hbm = pltpu.with_memory_space_constraint(reflectors, pltpu.HBM)
    keep, send = pl.pallas_call(
        gram_kernel,
        in_specs=[smem, vmem, hbm],
        out_specs=[vmem, vmem],
        out_shape=[jax.ShapeDtypeStruct((HALF // 2, packed), F32)] * 2,
        scratch_shapes=swept + [pltpu.VMEM((HALF, packed), F32), pltpu.SemaphoreType.DMA((SLOTS,))],
        compiler_params=params(20),
        cost_estimate=cost(6 * rows_dev * BLOCK * total, 4 * rows_dev * total),
        name="gram",
    )(place, lead, near_hbm)
    piece = scattered_sum(keep, send, 8)[None]
    pieces = join(received, piece, swap(piece, Z_LOW))
    pieces = join(*gather(pieces, Y_STEPS))
    pieces = gather(pieces, X_STEPS)
    pieces = pieces + [swap(piece, CORE) for piece in pieces]
    t_high, t_low = pl.pallas_call(
        inverse_kernel,
        in_specs=[smem] + [vmem] * 8,
        out_specs=[vmem] * 2,
        out_shape=[jax.ShapeDtypeStruct((total, total), BF16)] * 2,
        scratch_shapes=[pltpu.VMEM((total, total), F32), pltpu.VMEM((total, total), F32)],
        compiler_params=params(24),
        cost_estimate=cost(2 * total**3, 8 * total**2),
        name="inverse",
    )(place, *pieces)

    high, low, keep, send = pl.pallas_call(
        product_kernel,
        in_specs=[smem, vmem, vmem, hbm],
        out_specs=[vmem] * 4,
        out_shape=[held, held] + [jax.ShapeDtypeStruct((count // 2, total), F32)] * 2,
        scratch_shapes=swept + [pltpu.SemaphoreType.DMA((SLOTS,))],
        compiler_params=params(20),
        cost_estimate=cost(6 * rows_dev * count * total, 4 * rows_dev * total),
        name="product",
    )(place, lead, received, near_hbm)
    ordered = pl.pallas_call(
        reorder_kernel,
        in_specs=[vmem, vmem],
        out_specs=vmem,
        out_shape=jax.ShapeDtypeStruct((count, rows_dev), F32),
        compiler_params=params(16),
        cost_estimate=cost(6 * rows_dev * count * count, 16 * rows_dev * count),
        name="reorder",
    )(order, received)
    sums = gather(scattered_sum(keep, send, count // 8), X_STEPS)
    sums = sums + [swap(part, CORE) for part in sums]

    return pl.pallas_call(
        change_kernel,
        in_specs=[smem] + [vmem] * 14,
        out_specs=hbm,
        out_shape=jax.ShapeDtypeStruct((count, rows_dev), F32),
        scratch_shapes=[
            pltpu.VMEM((count, total), F32),
            pltpu.VMEM((2 * count, total), BF16),
            pltpu.VMEM((2, count, TILE), F32),
            pltpu.SemaphoreType.DMA((2,)),
        ],
        compiler_params=params(16),
        cost_estimate=cost(6 * rows_dev * count * total, 4 * rows_dev * count),
        name="change",
    )(place, order, *sums, t_high, t_low, ordered, high, low)


def solution(mesh):
    in_specs = (P(("row", "col"), None), P("col"), P("row", None), P())
    out_specs = P("col", "row")
    return jax.shard_map(per_device, mesh=mesh, in_specs=in_specs, out_specs=out_specs, check_vma=False)
```

```python
import jax
import jax.numpy as jnp
from jax import lax
from jax.experimental import pallas as pl
from jax.experimental.pallas import tpu as pltpu
from jax.sharding import PartitionSpec as P

F32 = jnp.float32
BF16 = jnp.bfloat16
TILE = 256
WIDE = 512
CHUNK = 16
SLOTS = 4
BLOCK = 128
HALF = 64
CORE, Z_HIGH, Z_LOW = 8, 16, 4
X_STEPS = (32, 96, 64)
Y_STEPS = (1, 3, 2)


def halves(x):
    high = x.astype(BF16)
    return high, (x - high.astype(F32)).astype(BF16)


def dot(a, b, ca=1, cb=0):
    return lax.dot_general(a, b, (((ca,), (cb,)), ((), ())), preferred_element_type=F32)


def dot3(a, b):
    m, n = a.shape[0], b.shape[1]
    both = dot(jnp.concatenate(halves(a), axis=0), jnp.concatenate(halves(b), axis=1))
    return both[:m, :n] + (both[:m, n:] + both[m:, :n])


def span(start, size):
    return pl.ds(start if isinstance(start, int) else pl.multiple_of(start, size), size)


def sweep(first, lead_ref, tiles_ref, slot_ref, even_ref, odd_ref, sem, put_sem, prepare, use, high_ref, low_ref):
    steps = tiles_ref.shape[0] // TILE
    total = tiles_ref.shape[1]
    index = lax.broadcasted_iota(jnp.int32, (CHUNK, total), 0)

    def fetch(step):
        slot = step % SLOTS if isinstance(step, int) else lax.rem(step, SLOTS)
        return pltpu.make_async_copy(tiles_ref.at[span(step * TILE, TILE), :], slot_ref.at[slot], sem.at[slot])

    def put(step, ref, at):
        part = span(step * TILE, TILE)
        return (
            pltpu.make_async_copy(ref.at[0], high_ref.at[part, :], put_sem.at[at, 0]),
            pltpu.make_async_copy(ref.at[1], low_ref.at[part, :], put_sem.at[at, 1]),
        )

    def halve(step, ref, quarter):
        slot = step % SLOTS if isinstance(step, int) else lax.rem(step, SLOTS)
        start = lead_ref[...] - (first + step * TILE)
        for at in range(quarter * TILE // 4, (quarter + 1) * TILE // 4, CHUNK):
            x = slot_ref[slot, at : at + CHUNK, :]
            lead = start - at
            x = jnp.where(index < lead, 0.0, jnp.where(index == lead, 1.0, x))
            high, low = halves(x)
            ref[0, at : at + CHUNK, :] = high
            ref[1, at : at + CHUNK, :] = low

    def work(step, now, later):
        left = prepare(step, now)
        for quarter in range(4):
            use(left, now, quarter)
            if later is not None:
                halve(step + 1, later, quarter)

    for step in range(SLOTS - 1):
        fetch(step).start()
    fetch(0).wait()
    for quarter in range(4):
        halve(0, even_ref, quarter)
    for copy in put(0, even_ref, 0):
        copy.start()

    @pl.loop(0, steps // 2 - 1)
    def _(pair):
        for step, now, later, at in ((2 * pair, even_ref, odd_ref, 1), (2 * pair + 1, odd_ref, even_ref, 0)):

            @pl.when(step + SLOTS - 1 < steps)
            def _():
                fetch(step + SLOTS - 1).start()

            @pl.when(step >= 1)
            def _():
                for copy in put(step - 1, later, at):
                    copy.wait()

            fetch(step + 1).wait()
            work(step, now, later)
            for copy in put(step + 1, later, at):
                copy.start()

    fetch(steps - 1).wait()
    for copy in put(steps - 3, odd_ref, 1):
        copy.wait()
    work(steps - 2, even_ref, odd_ref)
    for copy in put(steps - 1, odd_ref, 1):
        copy.start()
    work(steps - 1, odd_ref, None)
    for copy in put(steps - 2, even_ref, 0) + put(steps - 1, odd_ref, 1):
        copy.wait()


def add_product(sum_ref):
    count, total = sum_ref.shape
    part = total // 4

    def use(left, ref, quarter):
        at = slice(quarter * part, (quarter + 1) * part)
        both = dot(left, ref[0, :, at])
        sum_ref[:, at] += both[:count] + (both[count:] + dot(left[:count], ref[1, :, at]))

    return use


def gram_kernel(
    place_ref, lead_ref, tiles_ref, high_ref, low_ref, keep_ref, send_ref, slot_ref, even_ref, odd_ref, sum_ref, pack_ref, sem, put_sem
):
    total = tiles_ref.shape[1]
    first, core, x_at, col = place_ref[0], place_ref[1], place_ref[2], place_ref[3]
    lane_half = lax.broadcasted_iota(jnp.int32, (1, BLOCK), 1) // HALF
    turns = []
    for turn in (lax.rem(col, 4), 7 - lax.rem(col, 4)):
        parity = lax.rem(turn, 2)
        from_a = jnp.where(lane_half == parity, 1.0, 0.0).astype(BF16)
        from_b = jnp.where(lane_half == parity, 0.0, 1.0).astype(BF16)
        turns.append((parity, turn // 2, (15 - turn) // 2, from_a, from_b))

    def prepare(step, ref):
        def chosen(which, block_a, block_b, from_a, from_b):
            a = ref[which, :, span(block_a * BLOCK, BLOCK)]
            b = ref[which, :, span(block_b * BLOCK, BLOCK)]
            return a * from_a + b * from_b

        return jnp.concatenate([chosen(which, *turn[1:]) for which in (0, 1) for turn in turns], axis=1).T

    sum_ref[...] = jnp.zeros_like(sum_ref)
    sweep(
        first, lead_ref, tiles_ref, slot_ref, even_ref, odd_ref, sem, put_sem, prepare, add_product(sum_ref), high_ref, low_ref
    )

    for p, (parity, block_a, block_b, _, _) in enumerate(turns):
        pack_ref[p, :, :total] = sum_ref[span(p * BLOCK + (1 - parity) * HALF, HALF), :]
        for m in range(4):

            @pl.when(m <= block_a)
            def _():
                pack_ref[p, :, span((block_b + 1 + m) * BLOCK, BLOCK)] = sum_ref[
                    span(p * BLOCK + parity * HALF, HALF), m * BLOCK : (m + 1) * BLOCK
                ]

        for k in range(4):
            at = jnp.bitwise_xor(x_at, k) * 8
            to = slice(k * 16 + p * 8, k * 16 + p * 8 + 8)
            keep_ref[to, :] = pack_ref[p, span(core * 32 + at, 8), :]
            send_ref[to, :] = pack_ref[p, span((1 - core) * 32 + at, 8), :]


def product_copies(from_refs, to_refs, first, sem):
    rows = to_refs[0].shape[0]
    return [
        [
            pltpu.make_async_copy(a.at[first + at : first + at + WIDE, :], b.at[at : at + WIDE, :], sem.at[at // WIDE, i])
            for i, (a, b) in enumerate(zip(from_refs, to_refs))
        ]
        for at in range(0, rows, WIDE)
    ]


def product(vec_ref, from_refs, to_refs, first, sem, sum_ref, total):
    copies = product_copies(from_refs, to_refs, first, sem)
    count = vec_ref.shape[0]
    for pair in copies:
        for copy in pair:
            copy.start()
    for step, pair in enumerate(copies):
        at = step * WIDE
        left = jnp.concatenate(halves(vec_ref[:, first + at : first + at + WIDE]), axis=0)
        for copy in pair:
            copy.wait()
        both = dot(left, to_refs[0][at : at + WIDE, :])
        added = both[:count] + (both[count:] + dot(left[:count], to_refs[1][at : at + WIDE, :]))
        if total is not None:
            added = added + total[...]
        total = sum_ref
        sum_ref[...] = added


def first_product_kernel(_, vec_ref, from_high_ref, from_low_ref, high_ref, low_ref, sum_ref, sem):
    product(vec_ref, (from_high_ref, from_low_ref), (high_ref, low_ref), 0, sem, sum_ref, None)


def last_product_kernel(
    _, place_ref, total_ref, vec_ref, from_high_ref, from_low_ref, high_ref, low_ref, keep_ref, send_ref, sum_ref, sem
):
    first = vec_ref.shape[1] - high_ref.shape[0]
    product(vec_ref, (from_high_ref, from_low_ref), (high_ref, low_ref), first, sem, sum_ref, total_ref)
    core, x_at = place_ref[1], place_ref[2]
    for k in range(4):
        at = jnp.bitwise_xor(x_at, k) * 16
        keep_ref[k * 16 : k * 16 + 16, :] = sum_ref[span(core * 64 + at, 16), :]
        send_ref[k * 16 : k * 16 + 16, :] = sum_ref[span((1 - core) * 64 + at, 16), :]


def add_kernel(_, a_ref, b_ref, out_ref):
    out_ref[...] = a_ref[...] + b_ref[...]


def join_kernel(_, *refs):
    *parts, out_ref = refs
    at = 0
    for part in parts:
        out_ref[at : at + part.shape[0], :] = part[...]
        at += part.shape[0]


def sum_kernel(*refs):
    *parts, out_ref = refs
    a, b, c, d = (part[...] for part in parts)
    out_ref[...] = (a + b) + (c + d)


def reorder_kernel(order_ref, vec_ref, out_ref):
    order = order_ref[...]

    @pl.loop(0, vec_ref.shape[1] // WIDE)
    def _(step):
        part = span(step * WIDE, WIDE)
        value = vec_ref[:, part]
        v1 = value.astype(BF16)
        rest = value - v1.astype(F32)
        v2, v3 = halves(rest)
        out_ref[:, part] = dot(order, v1) + (dot(order, v2) + dot(order, v3))


def inverse_kernel(place_ref, *refs):
    *gram_refs, high_ref, low_ref, stage_ref, lower_ref, out_ref = refs
    total = out_ref.shape[0]
    blocks = total // BLOCK
    core, x_at, col = place_ref[1], place_ref[2], place_ref[3]
    r = lax.broadcasted_iota(jnp.int32, (BLOCK, BLOCK), 0)
    c = lax.broadcasted_iota(jnp.int32, (BLOCK, BLOCK), 1)
    for j in range(8):
        to = jnp.bitwise_xor(core, j // 4) * 4 + jnp.bitwise_xor(lax.rem(col, 4), j % 4)
        stage_ref[to] = gram_refs[j // 4][j % 4 * 64 : j % 4 * 64 + 64, :]
    for q in range(8):
        width = (q // 2 + 1) * BLOCK
        rest = 9 * BLOCK - width
        for k in range(8):
            at = jnp.bitwise_xor(x_at, k % 4) * 16 + q // 4 * 8
            piece = stage_ref[k // 4 * 4 + (q if q < 4 else 7 - q), span(at, 8), :]
            top, low = (15 - q) * HALF + k * 8, q * HALF + k * 8
            lower_ref[top : top + 8, :rest] = piece[:, :rest]
            lower_ref[low : low + 8, :width] = piece[:, rest:]
    out_ref[...] = jnp.zeros_like(out_ref)
    lows, inverses = [], []
    for q in range(blocks):
        part = pl.ds(q * BLOCK, BLOCK)
        square = lower_ref[part, part]
        lows.append(square)
        inverses.append(jnp.where(r == c, 2.0 / square, 0.0))
    same = r // HALF == c // HALF
    scales = [jnp.sum(inverses[q], axis=0, keepdims=True) for q in range(blocks)]
    scaled = [jnp.sum(inverses[q], axis=1, keepdims=True) for q in range(blocks)]
    powers = [jnp.where(same & (r > c), -lows[q] * scaled[q], 0.0) for q in range(blocks)]
    identity = jnp.where(r == c, 1.0, 0.0)
    products = [identity + powers[q] for q in range(blocks)]
    for _ in range(5):
        powers = [dot3(powers[q], powers[q]) for q in range(blocks)]
        products = [products[q] + dot3(products[q], powers[q]) for q in range(blocks)]
    inverses = [products[q] * scales[q] for q in range(blocks)]
    pair = (r >= HALF) & (c < HALF)
    mids = [dot3(jnp.where(pair, lows[q], 0.0), inverses[q]) for q in range(blocks)]
    inverses = [inverses[q] - dot3(inverses[q], mids[q]) for q in range(blocks)]
    size = BLOCK
    for q in range(blocks):
        part = pl.ds(q * BLOCK, BLOCK)
        out_ref[part, part] = inverses[q]
    while size < total:
        for start in range(0, total, 2 * size):
            a, b = pl.ds(start, size), pl.ds(start + size, size)
            mid = dot3(lower_ref[b, a], out_ref[a, a])
            out_ref[b, a] = -dot3(out_ref[b, b], mid)
        size *= 2
    high, low = halves(out_ref[...])
    high_ref[...] = high
    low_ref[...] = low


def change_kernel(place_ref, order_ref, *refs):
    mine_ref, other_ref, th_ref, tl_ref, vec_ref, *held_refs, out_ref, sum_ref, w_ref, put_ref, put_sem = refs
    count, rows = vec_ref.shape
    core, x_at = place_ref[1], place_ref[2]
    for k in range(4):
        at = jnp.bitwise_xor(x_at, k) * 16
        sum_ref[span(core * 64 + at, 16), :] = mine_ref[k * 16 : k * 16 + 16, :]
        sum_ref[span((1 - core) * 64 + at, 16), :] = other_ref[k * 16 : k * 16 + 16, :]
    yh, yl = halves(sum_ref[...])
    both = dot(jnp.concatenate([yh, yl], axis=0), th_ref[...])
    weighted = both[:count] + (both[count:] + dot(yh, tl_ref[...]))
    order = order_ref[...]
    wh, wl = halves(weighted)
    w_ref[:count, :] = dot(order, wh).astype(BF16)
    w_ref[count:, :] = dot(order, wl).astype(BF16)

    copies = []
    for step, at in enumerate(range(0, rows, WIDE)):
        part = slice(at, at + WIDE)
        split = held_refs[0].shape[0]
        high_ref, low_ref = held_refs[:2] if at < split else held_refs[2:]
        held = slice(at, at + WIDE) if at < split else slice(at - split, at - split + WIDE)
        both = dot(w_ref[...], high_ref[held, :], 1, 1)
        change = both[:count] + (both[count:] + dot(w_ref[:count, :], low_ref[held, :], 1, 1))
        put_ref[:, part] = vec_ref[:, part] - change
        copies.append(pltpu.make_async_copy(put_ref.at[:, part], out_ref.at[:, part], put_sem.at[step]))
        copies[-1].start()
    for copy in copies:
        copy.wait()


def params(mib):
    return pltpu.CompilerParams(vmem_limit_bytes=mib << 20)


def cost(flops, moved):
    return pl.CostEstimate(flops=flops, bytes_accessed=moved, transcendentals=0)


def swap(x, bits):
    return lax.ppermute(x, ("row", "col"), [(i, i ^ bits) for i in range(128)])


def gather(x, steps):
    near, far, across = (swap(x, bits) for bits in steps)
    return [x, near, across, far]


def small(kernel, shape, name, before, parts):
    after = [pl.BlockSpec(memory_space=pl.ANY)] * len(before)
    return pl.pallas_call(
        kernel,
        in_specs=after + [pl.BlockSpec(memory_space=pltpu.VMEM)] * len(parts),
        out_specs=pl.BlockSpec(memory_space=pltpu.VMEM),
        out_shape=jax.ShapeDtypeStruct(shape, F32),
        compiler_params=params(4),
        cost_estimate=cost(1 << 16, 1 << 16),
        name=name,
    )(*before, *parts)


def per_device(source_vectors, source_slot, reflectors, panel_offsets):
    row_count = lax.axis_size("row")
    col_count = lax.axis_size("col")
    src_block = source_vectors.shape[0]
    rows_dev, total = reflectors.shape
    width = total // panel_offsets.shape[0]
    count = src_block * row_count

    row = lax.axis_index("row")
    place = jnp.stack([row * rows_dev, row % 2, row // 4, lax.axis_index("col")]).astype(jnp.int32)
    lead = (panel_offsets[:, None] + jnp.arange(width, dtype=jnp.int32)[None, :]).reshape(1, total)
    placing = source_slot // (col_count * src_block) * src_block + source_slot % src_block
    order = (placing[:, None] == jnp.arange(count, dtype=jnp.int32)[None, :]).astype(BF16)

    smem = pl.BlockSpec(memory_space=pltpu.SMEM)
    vmem = pl.BlockSpec(memory_space=pltpu.VMEM)
    hbm = pl.BlockSpec(memory_space=pltpu.HBM)

    shaped = source_vectors.reshape(src_block, row_count, rows_dev).transpose(1, 0, 2)
    received = lax.all_to_all(shaped, "row", 0, 0, tiled=True).reshape(count, rows_dev)

    packed = 9 * BLOCK
    halved = pltpu.HBM((rows_dev, total), BF16)
    steps = rows_dev // WIDE
    high, low, keep, send = pl.pallas_call(
        gram_kernel,
        in_specs=[smem, vmem, hbm],
        out_specs=[hbm, hbm, vmem, vmem],
        out_shape=[halved, halved] + [jax.ShapeDtypeStruct((HALF, packed), F32)] * 2,
        scratch_shapes=[
            pltpu.VMEM((SLOTS, TILE, total), F32),
            pltpu.VMEM((2, TILE, total), BF16),
            pltpu.VMEM((2, TILE, total), BF16),
            pltpu.VMEM((2 * BLOCK, total), F32),
            pltpu.VMEM((2, HALF, packed), F32),
            pltpu.SemaphoreType.DMA((SLOTS,)),
            pltpu.SemaphoreType.DMA((2, 2)),
        ],
        compiler_params=params(20),
        cost_estimate=cost(12 * rows_dev * BLOCK * total, 8 * rows_dev * total),
        name="gram",
    )(place, lead, pltpu.with_memory_space_constraint(reflectors, pltpu.HBM))
    both = keep + swap(send, CORE)
    part = both[:16]
    for k, bits in ((1, 32), (3, 96), (2, 64)):
        part = part + swap(both[k * 16 : k * 16 + 16], bits)
    near = swap(part, Z_HIGH)

    after = pl.BlockSpec(memory_space=pl.ANY)
    high = pltpu.with_memory_space_constraint(high, pltpu.HBM)
    low = pltpu.with_memory_space_constraint(low, pltpu.HBM)
    split = steps // 2 * WIDE
    first_held, last_held = ([pltpu.VMEM((n, total), BF16)] * 2 for n in (split, rows_dev - split))
    summed = jax.ShapeDtypeStruct((count, total), F32)
    semaphores = pltpu.SemaphoreType.DMA((steps, 2))
    first_high, first_low, sums = pl.pallas_call(
        first_product_kernel,
        in_specs=[after, vmem, hbm, hbm],
        out_specs=[vmem] * 3,
        out_shape=first_held + [summed],
        scratch_shapes=[semaphores],
        compiler_params=params(8),
        cost_estimate=cost(3 * rows_dev * count * total, 2 * rows_dev * total),
        name="product_first",
    )(part, received, high, low)
    piece = small(add_kernel, (16, packed), "gram_z", [sums], [part, near])
    pieces = gather(piece, X_STEPS)
    last_high, last_low, keep, send = pl.pallas_call(
        last_product_kernel,
        in_specs=[after, smem, vmem, vmem, hbm, hbm],
        out_specs=[vmem] * 4,
        out_shape=last_held + [jax.ShapeDtypeStruct((count // 2, total), F32)] * 2,
        scratch_shapes=[pltpu.VMEM((count, total), F32), semaphores],
        compiler_params=params(8),
        cost_estimate=cost(3 * rows_dev * count * total, 2 * rows_dev * total),
        name="product_last",
    )(piece, place, sums, received, high, low)
    grams = small(join_kernel, (64, packed), "gram_x", [keep], pieces)
    pieces = gather(grams, Y_STEPS)

    ordered = pl.pallas_call(
        reorder_kernel,
        in_specs=[vmem, vmem],
        out_specs=vmem,
        out_shape=jax.ShapeDtypeStruct((count, rows_dev), F32),
        compiler_params=params(8),
        cost_estimate=cost(6 * rows_dev * count * count, 16 * rows_dev * count),
        name="reorder",
    )(order, received)
    both = small(add_kernel, (count // 2, total), "sum_core", [grams], [keep, swap(send, CORE)])
    parts = [both[: count // 8]]
    for k, bits in ((1, 32), (2, 64), (3, 96)):
        parts.append(swap(both[k * count // 8 : (k + 1) * count // 8], bits))
    sums = small(sum_kernel, (count // 8, total), "sum_x", [], parts)
    sums = small(add_kernel, (count // 8, total), "sum_z", [ordered], [sums, swap(sums, Z_HIGH)])
    mine = small(join_kernel, (count // 2, total), "sum_join", [ordered], gather(sums, X_STEPS))
    other = swap(mine, CORE)
    pieces = small(join_kernel, (256, packed), "gram_y", [mine], pieces)
    t_high, t_low = pl.pallas_call(
        inverse_kernel,
        in_specs=[smem] + [vmem] * 2,
        out_specs=[vmem] * 2,
        out_shape=[jax.ShapeDtypeStruct((total, total), BF16)] * 2,
        scratch_shapes=[
            pltpu.VMEM((8, 64, packed), F32),
            pltpu.VMEM((total, total), F32),
            pltpu.VMEM((total, total), F32),
        ],
        compiler_params=params(18),
        cost_estimate=cost(6 * total**3, 8 * total**2),
        name="inverse",
    )(place, pieces, swap(pieces, CORE))
    return pl.pallas_call(
        change_kernel,
        in_specs=[smem] + [vmem] * 10,
        out_specs=hbm,
        out_shape=jax.ShapeDtypeStruct((count, rows_dev), F32),
        scratch_shapes=[
            pltpu.VMEM((count, total), F32),
            pltpu.VMEM((2 * count, total), BF16),
            pltpu.VMEM((count, rows_dev), F32),
            pltpu.SemaphoreType.DMA((steps,)),
        ],
        compiler_params=params(12),
        cost_estimate=cost(6 * rows_dev * count * total, 4 * rows_dev * count),
        name="change",
    )(place, order, mine, other, t_high, t_low, ordered, first_high, first_low, last_high, last_low)


def solution(mesh):
    in_specs = (P(("row", "col"), None), P("col"), P("row", None), P())
    out_specs = P("col", "row")
    return jax.shard_map(per_device, mesh=mesh, in_specs=in_specs, out_specs=out_specs, check_vma=False)
```

```python
import jax
import jax.numpy as jnp
from jax import lax
from jax.experimental import pallas as pl
from jax.experimental.pallas import tpu as pltpu
from jax.sharding import PartitionSpec as P

F32 = jnp.float32
BF16 = jnp.bfloat16
TILE = 256
WIDE = 512
CHUNK = 16
SLOTS = 4
BLOCK = 128
HALF = 64
CORE, Z_HIGH, Z_LOW = 8, 16, 4
X_STEPS = (32, 96, 64)
Y_STEPS = (1, 3, 2)


def halves(x):
    high = x.astype(BF16)
    return high, (x - high.astype(F32)).astype(BF16)


def dot(a, b, ca=1, cb=0):
    return lax.dot_general(a, b, (((ca,), (cb,)), ((), ())), preferred_element_type=F32)


def dot3(a, b):
    m, n = a.shape[0], b.shape[1]
    both = dot(jnp.concatenate(halves(a), axis=0), jnp.concatenate(halves(b), axis=1))
    return both[:m, :n] + (both[:m, n:] + both[m:, :n])


def span(start, size):
    return pl.ds(start if isinstance(start, int) else pl.multiple_of(start, size), size)


def sweep(first, lead_ref, tiles_ref, slot_ref, even_ref, odd_ref, sem, put_sem, prepare, use, high_ref, low_ref):
    steps = tiles_ref.shape[0] // TILE
    total = tiles_ref.shape[1]
    index = lax.broadcasted_iota(jnp.int32, (CHUNK, total), 0)

    def fetch(step):
        slot = step % SLOTS if isinstance(step, int) else lax.rem(step, SLOTS)
        return pltpu.make_async_copy(tiles_ref.at[span(step * TILE, TILE), :], slot_ref.at[slot], sem.at[slot])

    def put(step, ref, at):
        part = span(step * TILE, TILE)
        return (
            pltpu.make_async_copy(ref.at[0], high_ref.at[part, :], put_sem.at[at, 0]),
            pltpu.make_async_copy(ref.at[1], low_ref.at[part, :], put_sem.at[at, 1]),
        )

    def halve(step, ref, quarter):
        slot = step % SLOTS if isinstance(step, int) else lax.rem(step, SLOTS)
        start = lead_ref[...] - (first + step * TILE)
        for at in range(quarter * TILE // 4, (quarter + 1) * TILE // 4, CHUNK):
            x = slot_ref[slot, at : at + CHUNK, :]
            lead = start - at
            x = jnp.where(index < lead, 0.0, jnp.where(index == lead, 1.0, x))
            high, low = halves(x)
            ref[0, at : at + CHUNK, :] = high
            ref[1, at : at + CHUNK, :] = low

    def work(step, now, later):
        left = prepare(step, now)
        for quarter in range(4):
            use(left, now, quarter)
            if later is not None:
                halve(step + 1, later, quarter)

    for step in range(SLOTS - 1):
        fetch(step).start()
    fetch(0).wait()
    for quarter in range(4):
        halve(0, even_ref, quarter)
    for copy in put(0, even_ref, 0):
        copy.start()

    @pl.loop(0, steps // 2 - 1)
    def _(pair):
        for step, now, later, at in ((2 * pair, even_ref, odd_ref, 1), (2 * pair + 1, odd_ref, even_ref, 0)):

            @pl.when(step + SLOTS - 1 < steps)
            def _():
                fetch(step + SLOTS - 1).start()

            @pl.when(step >= 1)
            def _():
                for copy in put(step - 1, later, at):
                    copy.wait()

            fetch(step + 1).wait()
            work(step, now, later)
            for copy in put(step + 1, later, at):
                copy.start()

    fetch(steps - 1).wait()
    for copy in put(steps - 3, odd_ref, 1):
        copy.wait()
    work(steps - 2, even_ref, odd_ref)
    for copy in put(steps - 1, odd_ref, 1):
        copy.start()
    work(steps - 1, odd_ref, None)
    for copy in put(steps - 2, even_ref, 0) + put(steps - 1, odd_ref, 1):
        copy.wait()


def add_product(sum_ref):
    count, total = sum_ref.shape
    part = total // 4

    def use(left, ref, quarter):
        at = slice(quarter * part, (quarter + 1) * part)
        both = dot(left, ref[0, :, at])
        sum_ref[:, at] += both[:count] + (both[count:] + dot(left[:count], ref[1, :, at]))

    return use


def gram_kernel(
    place_ref, lead_ref, tiles_ref, high_ref, low_ref, keep_ref, send_ref, slot_ref, even_ref, odd_ref, sum_ref, pack_ref, sem, put_sem
):
    total = tiles_ref.shape[1]
    first, core, x_at, col = place_ref[0], place_ref[1], place_ref[2], place_ref[3]
    lane_half = lax.broadcasted_iota(jnp.int32, (1, BLOCK), 1) // HALF
    turns = []
    for turn in (lax.rem(col, 4), 7 - lax.rem(col, 4)):
        parity = lax.rem(turn, 2)
        from_a = jnp.where(lane_half == parity, 1.0, 0.0).astype(BF16)
        from_b = jnp.where(lane_half == parity, 0.0, 1.0).astype(BF16)
        turns.append((parity, turn // 2, (15 - turn) // 2, from_a, from_b))

    def prepare(step, ref):
        def chosen(which, block_a, block_b, from_a, from_b):
            a = ref[which, :, span(block_a * BLOCK, BLOCK)]
            b = ref[which, :, span(block_b * BLOCK, BLOCK)]
            return a * from_a + b * from_b

        return jnp.concatenate([chosen(which, *turn[1:]) for which in (0, 1) for turn in turns], axis=1).T

    sum_ref[...] = jnp.zeros_like(sum_ref)
    sweep(
        first, lead_ref, tiles_ref, slot_ref, even_ref, odd_ref, sem, put_sem, prepare, add_product(sum_ref), high_ref, low_ref
    )

    for p, (parity, block_a, block_b, _, _) in enumerate(turns):
        pack_ref[p, :, :total] = sum_ref[span(p * BLOCK + (1 - parity) * HALF, HALF), :]
        for m in range(4):

            @pl.when(m <= block_a)
            def _():
                pack_ref[p, :, span((block_b + 1 + m) * BLOCK, BLOCK)] = sum_ref[
                    span(p * BLOCK + parity * HALF, HALF), m * BLOCK : (m + 1) * BLOCK
                ]

        for k in range(4):
            at = jnp.bitwise_xor(x_at, k) * 8
            to = slice(k * 16 + p * 8, k * 16 + p * 8 + 8)
            keep_ref[to, :] = pack_ref[p, span(core * 32 + at, 8), :]
            send_ref[to, :] = pack_ref[p, span((1 - core) * 32 + at, 8), :]


def product_copies(from_refs, to_refs, first, sem):
    rows = to_refs[0].shape[0]
    return [
        [
            pltpu.make_async_copy(a.at[first + at : first + at + WIDE, :], b.at[at : at + WIDE, :], sem.at[at // WIDE, i])
            for i, (a, b) in enumerate(zip(from_refs, to_refs))
        ]
        for at in range(0, rows, WIDE)
    ]


def product(vec_ref, from_refs, to_refs, first, sem, sum_ref, total):
    copies = product_copies(from_refs, to_refs, first, sem)
    count = vec_ref.shape[0]
    for pair in copies:
        for copy in pair:
            copy.start()
    for step, pair in enumerate(copies):
        at = step * WIDE
        left = jnp.concatenate(halves(vec_ref[:, first + at : first + at + WIDE]), axis=0)
        for copy in pair:
            copy.wait()
        both = dot(left, to_refs[0][at : at + WIDE, :])
        added = both[:count] + (both[count:] + dot(left[:count], to_refs[1][at : at + WIDE, :]))
        if total is not None:
            added = added + total[...]
        total = sum_ref
        sum_ref[...] = added


def first_product_kernel(_, vec_ref, from_high_ref, from_low_ref, high_ref, low_ref, sum_ref, sem):
    product(vec_ref, (from_high_ref, from_low_ref), (high_ref, low_ref), 0, sem, sum_ref, None)


def last_product_kernel(
    _, place_ref, total_ref, vec_ref, from_high_ref, from_low_ref, high_ref, low_ref, out_ref, sum_ref, sem
):
    first = vec_ref.shape[1] - high_ref.shape[0]
    product(vec_ref, (from_high_ref, from_low_ref), (high_ref, low_ref), first, sem, sum_ref, total_ref)
    core, x_at = place_ref[1], place_ref[2]
    for k in range(8):
        at = jnp.bitwise_xor(core, k // 4) * 64 + jnp.bitwise_xor(x_at, k % 4) * 16
        out_ref[k * 16 : k * 16 + 16, :] = sum_ref[span(at, 16), :]


def split_kernel(_, sum_ref, send_ref):
    send_ref[...] = sum_ref[send_ref.shape[0] :, :]


def add_kernel(*refs):
    *_, a_ref, b_ref, out_ref = refs
    out_ref[...] = a_ref[: b_ref.shape[0], :] + b_ref[...]


def join_kernel(_, *refs):
    *parts, out_ref = refs
    at = 0
    for part in parts:
        out_ref[at : at + part.shape[0], :] = part[...]
        at += part.shape[0]


def sum_kernel(_, *refs):
    *parts, out_ref = refs
    a, b, c, d = (part[...] for part in parts)
    out_ref[...] = (a + b) + (c + d)


def reorder_kernel(order_ref, vec_ref, out_ref):
    order = order_ref[...]

    @pl.loop(0, vec_ref.shape[1] // WIDE)
    def _(step):
        part = span(step * WIDE, WIDE)
        value = vec_ref[:, part]
        v1 = value.astype(BF16)
        rest = value - v1.astype(F32)
        v2, v3 = halves(rest)
        out_ref[:, part] = dot(order, v1) + (dot(order, v2) + dot(order, v3))


def blocks_kernel(place_ref, *refs):
    *gram_refs, lower_ref, blocks_ref, stage_ref = refs
    total = lower_ref.shape[0]
    blocks = total // BLOCK
    core, x_at, col = place_ref[1], place_ref[2], place_ref[3]
    r = lax.broadcasted_iota(jnp.int32, (BLOCK, BLOCK), 0)
    c = lax.broadcasted_iota(jnp.int32, (BLOCK, BLOCK), 1)
    for j in range(8):
        to = jnp.bitwise_xor(core, j // 4) * 4 + jnp.bitwise_xor(lax.rem(col, 4), j % 4)
        stage_ref[to] = gram_refs[j // 4][j % 4 * 64 : j % 4 * 64 + 64, :]
    for q in range(8):
        width = (q // 2 + 1) * BLOCK
        rest = 9 * BLOCK - width
        for k in range(8):
            at = jnp.bitwise_xor(x_at, k % 4) * 16 + q // 4 * 8
            piece = stage_ref[k // 4 * 4 + (q if q < 4 else 7 - q), span(at, 8), :]
            top, low = (15 - q) * HALF + k * 8, q * HALF + k * 8
            lower_ref[top : top + 8, :rest] = piece[:, :rest]
            lower_ref[low : low + 8, :width] = piece[:, rest:]
    lows, inverses = [], []
    for q in range(blocks):
        part = pl.ds(q * BLOCK, BLOCK)
        square = lower_ref[part, part]
        lows.append(square)
        inverses.append(jnp.where(r == c, 2.0 / square, 0.0))
    same = r // HALF == c // HALF
    scales = [jnp.sum(inverses[q], axis=0, keepdims=True) for q in range(blocks)]
    scaled = [jnp.sum(inverses[q], axis=1, keepdims=True) for q in range(blocks)]
    powers = [jnp.where(same & (r > c), -lows[q] * scaled[q], 0.0) for q in range(blocks)]
    identity = jnp.where(r == c, 1.0, 0.0)
    products = [identity + powers[q] for q in range(blocks)]
    for _ in range(5):
        powers = [dot3(powers[q], powers[q]) for q in range(blocks)]
        products = [products[q] + dot3(products[q], powers[q]) for q in range(blocks)]
    inverses = [products[q] * scales[q] for q in range(blocks)]
    pair = (r >= HALF) & (c < HALF)
    mids = [dot3(jnp.where(pair, lows[q], 0.0), inverses[q]) for q in range(blocks)]
    inverses = [inverses[q] - dot3(inverses[q], mids[q]) for q in range(blocks)]
    for q in range(blocks):
        blocks_ref[q] = inverses[q]


def inverse_kernel(lower_ref, blocks_ref, th_ref, tl_ref, lh_ref, ll_ref, out_ref):
    total = lower_ref.shape[0]
    half = total // 2
    for start in range(0, total, 2 * BLOCK):
        at = start % half
        a, b = slice(start, start + BLOCK), slice(start + BLOCK, start + 2 * BLOCK)
        ac, bc = slice(at, at + BLOCK), slice(at + BLOCK, at + 2 * BLOCK)
        first, last = blocks_ref[start // BLOCK], blocks_ref[start // BLOCK + 1]
        out_ref[a, ac] = first
        out_ref[b, bc] = last
        out_ref[a, bc] = jnp.zeros((BLOCK, BLOCK), F32)
        out_ref[b, ac] = -dot3(last, dot3(lower_ref[b, a], first))
    quarter = half // 2
    for start in (0, half):
        a, b = slice(start, start + quarter), slice(start + quarter, start + half)
        out_ref[a, quarter:] = jnp.zeros((quarter, quarter), F32)
        out_ref[b, :quarter] = -dot3(out_ref[b, quarter:], dot3(lower_ref[b, a], out_ref[a, :quarter]))
    th_ref[...], tl_ref[...] = halves(out_ref[...])
    lh_ref[...], ll_ref[...] = halves(lower_ref[half:, :half])


def change_kernel(place_ref, order_ref, *refs):
    mine_ref, other_ref, th_ref, tl_ref, lh_ref, ll_ref, vec_ref, *held_refs, out_ref, sum_ref, w_ref, put_ref, put_sem = refs
    count, rows = vec_ref.shape
    core, x_at = place_ref[1], place_ref[2]
    for k in range(4):
        at = jnp.bitwise_xor(x_at, k) * 16
        sum_ref[span(core * 64 + at, 16), :] = mine_ref[k * 16 : k * 16 + 16, :]
        sum_ref[span((1 - core) * 64 + at, 16), :] = other_ref[k * 16 : k * 16 + 16, :]
    def times(x, high, low):
        xh, xl = halves(x)
        both = dot(jnp.concatenate([xh, xl], axis=0), high)
        return both[:count] + (both[count:] + dot(xh, low))

    half = sum_ref.shape[1] // 2
    order = order_ref[...]
    last = times(sum_ref[:, half:], th_ref[half:, :], tl_ref[half:, :])
    first = sum_ref[:, :half] - times(last, lh_ref[...], ll_ref[...])
    first = times(first, th_ref[:half, :], tl_ref[:half, :])
    for at, part in ((0, first), (half, last)):
        wh, wl = halves(part)
        w_ref[:count, at : at + half] = dot(order, wh).astype(BF16)
        w_ref[count:, at : at + half] = dot(order, wl).astype(BF16)

    copies = []
    for step, at in enumerate(range(0, rows, WIDE)):
        part = slice(at, at + WIDE)
        split = held_refs[0].shape[0]
        high_ref, low_ref = held_refs[:2] if at < split else held_refs[2:]
        held = slice(at, at + WIDE) if at < split else slice(at - split, at - split + WIDE)
        both = dot(w_ref[...], high_ref[held, :], 1, 1)
        change = both[:count] + (both[count:] + dot(w_ref[:count, :], low_ref[held, :], 1, 1))
        put_ref[:, part] = vec_ref[:, part] - change
        copies.append(pltpu.make_async_copy(put_ref.at[:, part], out_ref.at[:, part], put_sem.at[step]))
        copies[-1].start()
    for copy in copies:
        copy.wait()


def params(mib):
    return pltpu.CompilerParams(vmem_limit_bytes=mib << 20)


def cost(flops, moved):
    return pl.CostEstimate(flops=flops, bytes_accessed=moved, transcendentals=0)


def swap(x, bits):
    return lax.ppermute(x, ("row", "col"), [(i, i ^ bits) for i in range(128)])


def gather(x, steps):
    across, far, near = (swap(x, bits) for bits in reversed(steps))
    return [x, near, across, far]


def small(kernel, shape, name, before, parts):
    after = [pl.BlockSpec(memory_space=pl.ANY)] * len(before)
    return pl.pallas_call(
        kernel,
        in_specs=after + [pl.BlockSpec(memory_space=pltpu.VMEM)] * len(parts),
        out_specs=pl.BlockSpec(memory_space=pltpu.VMEM),
        out_shape=jax.ShapeDtypeStruct(shape, F32),
        compiler_params=params(4),
        cost_estimate=cost(1 << 16, 1 << 16),
        name=name,
    )(*before, *parts)


def per_device(source_vectors, source_slot, reflectors, panel_offsets):
    row_count = lax.axis_size("row")
    col_count = lax.axis_size("col")
    src_block = source_vectors.shape[0]
    rows_dev, total = reflectors.shape
    width = total // panel_offsets.shape[0]
    count = src_block * row_count

    row = lax.axis_index("row")
    place = jnp.stack([row * rows_dev, row % 2, row // 4, lax.axis_index("col")]).astype(jnp.int32)
    lead = (panel_offsets[:, None] + jnp.arange(width, dtype=jnp.int32)[None, :]).reshape(1, total)
    placing = source_slot // (col_count * src_block) * src_block + source_slot % src_block
    order = (placing[:, None] == jnp.arange(count, dtype=jnp.int32)[None, :]).astype(BF16)

    smem = pl.BlockSpec(memory_space=pltpu.SMEM)
    vmem = pl.BlockSpec(memory_space=pltpu.VMEM)
    hbm = pl.BlockSpec(memory_space=pltpu.HBM)

    shaped = source_vectors.reshape(src_block, row_count, rows_dev).transpose(1, 0, 2)
    received = lax.all_to_all(shaped, "row", 0, 0, tiled=True).reshape(count, rows_dev)

    packed = 9 * BLOCK
    halved = pltpu.HBM((rows_dev, total), BF16)
    steps = rows_dev // WIDE
    high, low, keep, send = pl.pallas_call(
        gram_kernel,
        in_specs=[smem, vmem, hbm],
        out_specs=[hbm, hbm, vmem, vmem],
        out_shape=[halved, halved] + [jax.ShapeDtypeStruct((HALF, packed), F32)] * 2,
        scratch_shapes=[
            pltpu.VMEM((SLOTS, TILE, total), F32),
            pltpu.VMEM((2, TILE, total), BF16),
            pltpu.VMEM((2, TILE, total), BF16),
            pltpu.VMEM((2 * BLOCK, total), F32),
            pltpu.VMEM((2, HALF, packed), F32),
            pltpu.SemaphoreType.DMA((SLOTS,)),
            pltpu.SemaphoreType.DMA((2, 2)),
        ],
        compiler_params=params(20),
        cost_estimate=cost(12 * rows_dev * BLOCK * total, 8 * rows_dev * total),
        name="gram",
    )(place, lead, pltpu.with_memory_space_constraint(reflectors, pltpu.HBM))
    both = keep + swap(send, CORE)
    part = both[:16]
    for k, bits in ((1, 32), (3, 96), (2, 64)):
        part = part + swap(both[k * 16 : k * 16 + 16], bits)
    near = swap(part, Z_HIGH)

    after = pl.BlockSpec(memory_space=pl.ANY)
    high = pltpu.with_memory_space_constraint(high, pltpu.HBM)
    low = pltpu.with_memory_space_constraint(low, pltpu.HBM)
    split = (steps + 1) // 2 * WIDE
    first_held, last_held = ([pltpu.VMEM((n, total), BF16)] * 2 for n in (split, rows_dev - split))
    summed = jax.ShapeDtypeStruct((count, total), F32)
    semaphores = pltpu.SemaphoreType.DMA((steps, 2))
    first_high, first_low, sums = pl.pallas_call(
        first_product_kernel,
        in_specs=[after, vmem, hbm, hbm],
        out_specs=[vmem] * 3,
        out_shape=first_held + [summed],
        scratch_shapes=[semaphores],
        compiler_params=params(8),
        cost_estimate=cost(3 * rows_dev * count * total, 2 * rows_dev * total),
        name="product_first",
    )(part, received, high, low)
    piece = small(add_kernel, (16, packed), "gram_z", [sums], [part, near])
    pieces = gather(piece, X_STEPS)
    last_high, last_low, sums = pl.pallas_call(
        last_product_kernel,
        in_specs=[after, smem, vmem, vmem, hbm, hbm],
        out_specs=[vmem] * 3,
        out_shape=last_held + [summed],
        scratch_shapes=[pltpu.VMEM((count, total), F32), semaphores],
        compiler_params=params(8),
        cost_estimate=cost(3 * rows_dev * count * total, 2 * rows_dev * total),
        name="product_last",
    )(piece, place, sums, received, high, low)
    grams = small(join_kernel, (64, packed), "gram_x", [sums], pieces)
    pieces = gather(grams, Y_STEPS)
    send = small(split_kernel, (count // 2, total), "sum_split", [grams], [sums])
    ordered = pl.pallas_call(
        reorder_kernel,
        in_specs=[vmem, vmem],
        out_specs=vmem,
        out_shape=jax.ShapeDtypeStruct((count, rows_dev), F32),
        compiler_params=params(8),
        cost_estimate=cost(6 * rows_dev * count * count, 16 * rows_dev * count),
        name="reorder",
    )(order, received)
    both = small(add_kernel, (count // 2, total), "sum_core", [grams], [sums, swap(send, CORE)])
    parts = [both[: count // 8]]
    for k, bits in ((1, 32), (2, 64), (3, 96)):
        parts.append(swap(both[k * count // 8 : (k + 1) * count // 8], bits))
    sums = small(sum_kernel, (count // 8, total), "sum_x", [pieces[1]], parts)
    sums = small(add_kernel, (count // 8, total), "sum_z", [ordered], [sums, swap(sums, Z_HIGH)])
    before_y = sums
    sums = gather(sums, X_STEPS)
    grams = small(join_kernel, (256, packed), "gram_y", [before_y], pieces)
    lower, blocks = pl.pallas_call(
        blocks_kernel,
        in_specs=[smem] + [vmem] * 2,
        out_specs=[vmem] * 2,
        out_shape=[jax.ShapeDtypeStruct((total, total), F32), jax.ShapeDtypeStruct((total // BLOCK, BLOCK, BLOCK), F32)],
        scratch_shapes=[pltpu.VMEM((8, 64, packed), F32)],
        compiler_params=params(12),
        cost_estimate=cost(4 * total**3, 4 * total**2),
        name="inverse_blocks",
    )(place, grams, swap(grams, CORE))
    mine = small(join_kernel, (count // 2, total), "sum_join", [blocks], sums)
    other = swap(mine, CORE)
    inverses = pl.pallas_call(
        inverse_kernel,
        in_specs=[vmem] * 2,
        out_specs=[vmem] * 4,
        out_shape=[jax.ShapeDtypeStruct((total, total // 2), BF16)] * 2 + [jax.ShapeDtypeStruct((total // 2, total // 2), BF16)] * 2,
        scratch_shapes=[pltpu.VMEM((total, total // 2), F32)],
        compiler_params=params(12),
        cost_estimate=cost(4 * total**3, 4 * total**2),
        name="inverse",
    )(lower, blocks)

    return pl.pallas_call(
        change_kernel,
        in_specs=[smem] + [vmem] * 12,
        out_specs=hbm,
        out_shape=jax.ShapeDtypeStruct((count, rows_dev), F32),
        scratch_shapes=[
            pltpu.VMEM((count, total), F32),
            pltpu.VMEM((2 * count, total), BF16),
            pltpu.VMEM((count, rows_dev), F32),
            pltpu.SemaphoreType.DMA((steps,)),
        ],
        compiler_params=params(12),
        cost_estimate=cost(6 * rows_dev * count * total, 4 * rows_dev * count),
        name="change",
    )(place, order, mine, other, *inverses, ordered, first_high, first_low, last_high, last_low)


def solution(mesh):
    in_specs = (P(("row", "col"), None), P("col"), P("row", None), P())
    out_specs = P("col", "row")
    return jax.shard_map(per_device, mesh=mesh, in_specs=in_specs, out_specs=out_specs, check_vma=False)
```

```python
import jax
import jax.numpy as jnp
from jax import lax
from jax.experimental import pallas as pl
from jax.experimental.pallas import tpu as pltpu
from jax.sharding import PartitionSpec as P

F32 = jnp.float32
BF16 = jnp.bfloat16
TILE = 256
WIDE = 512
CHUNK = 16
SLOTS = 4
BLOCK = 128
HALF = 64
CORE, Z_HIGH, Z_LOW = 8, 16, 4
X_STEPS = (32, 96, 64)
Y_STEPS = (1, 3, 2)


def halves(x):
    high = x.astype(BF16)
    return high, (x - high.astype(F32)).astype(BF16)


def dot(a, b, ca=1, cb=0):
    return lax.dot_general(a, b, (((ca,), (cb,)), ((), ())), preferred_element_type=F32)


def dot3(a, b):
    m, n = a.shape[0], b.shape[1]
    both = dot(jnp.concatenate(halves(a), axis=0), jnp.concatenate(halves(b), axis=1))
    return both[:m, :n] + (both[:m, n:] + both[m:, :n])


def span(start, size):
    return pl.ds(start if isinstance(start, int) else pl.multiple_of(start, size), size)


def sweep(first, lead_ref, tiles_ref, slot_ref, even_ref, odd_ref, sem, put_sem, prepare, use, high_ref, low_ref):
    steps = tiles_ref.shape[0] // TILE
    total = tiles_ref.shape[1]
    index = lax.broadcasted_iota(jnp.int32, (CHUNK, total), 0)

    def fetch(step):
        slot = step % SLOTS if isinstance(step, int) else lax.rem(step, SLOTS)
        return pltpu.make_async_copy(tiles_ref.at[span(step * TILE, TILE), :], slot_ref.at[slot], sem.at[slot])

    def put(step, ref, at):
        part = span(step * TILE, TILE)
        return (
            pltpu.make_async_copy(ref.at[0], high_ref.at[part, :], put_sem.at[at, 0]),
            pltpu.make_async_copy(ref.at[1], low_ref.at[part, :], put_sem.at[at, 1]),
        )

    def halve(step, ref, quarter):
        slot = step % SLOTS if isinstance(step, int) else lax.rem(step, SLOTS)
        start = lead_ref[...] - (first + step * TILE)
        for at in range(quarter * TILE // 4, (quarter + 1) * TILE // 4, CHUNK):
            x = slot_ref[slot, at : at + CHUNK, :]
            lead = start - at
            x = jnp.where(index < lead, 0.0, jnp.where(index == lead, 1.0, x))
            high, low = halves(x)
            ref[0, at : at + CHUNK, :] = high
            ref[1, at : at + CHUNK, :] = low

    def work(step, now, later):
        left = prepare(step, now)
        for quarter in range(4):
            use(left, now, quarter)
            if later is not None:
                halve(step + 1, later, quarter)

    for step in range(SLOTS - 1):
        fetch(step).start()
    fetch(0).wait()
    for quarter in range(4):
        halve(0, even_ref, quarter)
    for copy in put(0, even_ref, 0):
        copy.start()

    @pl.loop(0, steps // 2 - 1)
    def _(pair):
        for step, now, later, at in ((2 * pair, even_ref, odd_ref, 1), (2 * pair + 1, odd_ref, even_ref, 0)):

            @pl.when(step + SLOTS - 1 < steps)
            def _():
                fetch(step + SLOTS - 1).start()

            @pl.when(step >= 1)
            def _():
                for copy in put(step - 1, later, at):
                    copy.wait()

            fetch(step + 1).wait()
            work(step, now, later)
            for copy in put(step + 1, later, at):
                copy.start()

    fetch(steps - 1).wait()
    for copy in put(steps - 3, odd_ref, 1):
        copy.wait()
    work(steps - 2, even_ref, odd_ref)
    for copy in put(steps - 1, odd_ref, 1):
        copy.start()
    work(steps - 1, odd_ref, None)
    for copy in put(steps - 2, even_ref, 0) + put(steps - 1, odd_ref, 1):
        copy.wait()


def add_product(sum_ref):
    count, total = sum_ref.shape
    part = total // 4

    def use(left, ref, quarter):
        at = slice(quarter * part, (quarter + 1) * part)
        both = dot(left, ref[0, :, at])
        sum_ref[:, at] += both[:count] + (both[count:] + dot(left[:count], ref[1, :, at]))

    return use


def gram_kernel(
    place_ref, lead_ref, tiles_ref, high_ref, low_ref, keep_ref, send_ref, slot_ref, even_ref, odd_ref, sum_ref, pack_ref, sem, put_sem
):
    total = tiles_ref.shape[1]
    first, core, x_at, col = place_ref[0], place_ref[1], place_ref[2], place_ref[3]
    lane_half = lax.broadcasted_iota(jnp.int32, (1, BLOCK), 1) // HALF
    turns = []
    for turn in (lax.rem(col, 4), 7 - lax.rem(col, 4)):
        parity = lax.rem(turn, 2)
        from_a = jnp.where(lane_half == parity, 1.0, 0.0).astype(BF16)
        from_b = jnp.where(lane_half == parity, 0.0, 1.0).astype(BF16)
        turns.append((parity, turn // 2, (15 - turn) // 2, from_a, from_b))

    def prepare(step, ref):
        def chosen(which, block_a, block_b, from_a, from_b):
            a = ref[which, :, span(block_a * BLOCK, BLOCK)]
            b = ref[which, :, span(block_b * BLOCK, BLOCK)]
            return a * from_a + b * from_b

        return jnp.concatenate([chosen(which, *turn[1:]) for which in (0, 1) for turn in turns], axis=1).T

    sum_ref[...] = jnp.zeros_like(sum_ref)
    sweep(
        first, lead_ref, tiles_ref, slot_ref, even_ref, odd_ref, sem, put_sem, prepare, add_product(sum_ref), high_ref, low_ref
    )

    for p, (parity, block_a, block_b, _, _) in enumerate(turns):
        pack_ref[p, :, :total] = sum_ref[span(p * BLOCK + (1 - parity) * HALF, HALF), :]
        for m in range(4):

            @pl.when(m <= block_a)
            def _():
                pack_ref[p, :, span((block_b + 1 + m) * BLOCK, BLOCK)] = sum_ref[
                    span(p * BLOCK + parity * HALF, HALF), m * BLOCK : (m + 1) * BLOCK
                ]

        for k in range(4):
            at = jnp.bitwise_xor(x_at, k) * 8
            to = slice(k * 16 + p * 8, k * 16 + p * 8 + 8)
            keep_ref[to, :] = pack_ref[p, span(core * 32 + at, 8), :]
            send_ref[to, :] = pack_ref[p, span((1 - core) * 32 + at, 8), :]


def product_copies(from_refs, to_refs, first, sem):
    rows = to_refs[0].shape[0]
    return [
        [
            pltpu.make_async_copy(a.at[first + at : first + at + WIDE, :], b.at[at : at + WIDE, :], sem.at[at // WIDE, i])
            for i, (a, b) in enumerate(zip(from_refs, to_refs))
        ]
        for at in range(0, rows, WIDE)
    ]


def product(vec_ref, from_refs, to_refs, first, sem, sum_ref, total):
    copies = product_copies(from_refs, to_refs, first, sem)
    count = vec_ref.shape[0]
    for pair in copies:
        for copy in pair:
            copy.start()
    for step, pair in enumerate(copies):
        at = step * WIDE
        left = jnp.concatenate(halves(vec_ref[:, first + at : first + at + WIDE]), axis=0)
        for copy in pair:
            copy.wait()
        both = dot(left, to_refs[0][at : at + WIDE, :])
        added = both[:count] + (both[count:] + dot(left[:count], to_refs[1][at : at + WIDE, :]))
        if total is not None:
            added = added + total[...]
        total = sum_ref
        sum_ref[...] = added


def first_product_kernel(_, vec_ref, from_high_ref, from_low_ref, high_ref, low_ref, sum_ref, sem):
    product(vec_ref, (from_high_ref, from_low_ref), (high_ref, low_ref), 0, sem, sum_ref, None)


def last_product_kernel(
    _, place_ref, total_ref, vec_ref, from_high_ref, from_low_ref, high_ref, low_ref, out_ref, sum_ref, sem
):
    first = vec_ref.shape[1] - high_ref.shape[0]
    product(vec_ref, (from_high_ref, from_low_ref), (high_ref, low_ref), first, sem, sum_ref, total_ref)
    core, x_at = place_ref[1], place_ref[2]
    for k in range(8):
        at = jnp.bitwise_xor(core, k // 4) * 64 + jnp.bitwise_xor(x_at, k % 4) * 16
        out_ref[k * 16 : k * 16 + 16, :] = sum_ref[span(at, 16), :]


def split_kernel(_, sum_ref, send_ref):
    send_ref[...] = sum_ref[send_ref.shape[0] :, :]


def add_kernel(*refs):
    *_, a_ref, b_ref, out_ref = refs
    out_ref[...] = a_ref[: b_ref.shape[0], :] + b_ref[...]


def join_kernel(_, *refs):
    *parts, out_ref = refs
    at = 0
    for part in parts:
        out_ref[at : at + part.shape[0], :] = part[...]
        at += part.shape[0]


def sum_kernel(_, *refs):
    *parts, out_ref = refs
    a, b, c, d = (part[...] for part in parts)
    out_ref[...] = (a + b) + (c + d)


def reorder_kernel(order_ref, vec_ref, out_ref):
    order = order_ref[...]

    @pl.loop(0, vec_ref.shape[1] // WIDE)
    def _(step):
        part = span(step * WIDE, WIDE)
        value = vec_ref[:, part]
        v1 = value.astype(BF16)
        rest = value - v1.astype(F32)
        v2, v3 = halves(rest)
        out_ref[:, part] = dot(order, v1) + (dot(order, v2) + dot(order, v3))


def blocks_kernel(place_ref, *refs):
    *gram_refs, lower_ref, blocks_ref, stage_ref = refs
    total = lower_ref.shape[0]
    blocks = total // BLOCK
    core, x_at, col = place_ref[1], place_ref[2], place_ref[3]
    r = lax.broadcasted_iota(jnp.int32, (BLOCK, BLOCK), 0)
    c = lax.broadcasted_iota(jnp.int32, (BLOCK, BLOCK), 1)
    for j in range(8):
        to = jnp.bitwise_xor(core, j // 4) * 4 + jnp.bitwise_xor(lax.rem(col, 4), j % 4)
        stage_ref[to] = gram_refs[j // 4][j % 4 * 64 : j % 4 * 64 + 64, :]
    for q in range(8):
        width = (q // 2 + 1) * BLOCK
        rest = 9 * BLOCK - width
        for k in range(8):
            at = jnp.bitwise_xor(x_at, k % 4) * 16 + q // 4 * 8
            piece = stage_ref[k // 4 * 4 + (q if q < 4 else 7 - q), span(at, 8), :]
            top, low = (15 - q) * HALF + k * 8, q * HALF + k * 8
            lower_ref[top : top + 8, :rest] = piece[:, :rest]
            lower_ref[low : low + 8, :width] = piece[:, rest:]
    lows, inverses = [], []
    for q in range(blocks):
        part = pl.ds(q * BLOCK, BLOCK)
        square = lower_ref[part, part]
        lows.append(square)
        inverses.append(jnp.where(r == c, 2.0 / square, 0.0))
    same = r // HALF == c // HALF
    scales = [jnp.sum(inverses[q], axis=0, keepdims=True) for q in range(blocks)]
    scaled = [jnp.sum(inverses[q], axis=1, keepdims=True) for q in range(blocks)]
    powers = [jnp.where(same & (r > c), -lows[q] * scaled[q], 0.0) for q in range(blocks)]
    identity = jnp.where(r == c, 1.0, 0.0)
    products = [identity + powers[q] for q in range(blocks)]
    powers = [dot3(power, power) for power in powers]
    for _ in range(4):
        both = [dot3(jnp.concatenate([powers[q], products[q]], axis=0), powers[q]) for q in range(blocks)]
        powers = [part[:BLOCK] for part in both]
        products = [products[q] + both[q][BLOCK:] for q in range(blocks)]
    products = [products[q] + dot3(products[q], powers[q]) for q in range(blocks)]
    inverses = [products[q] * scales[q] for q in range(blocks)]
    pair = (r >= HALF) & (c < HALF)
    mids = [dot3(jnp.where(pair, lows[q], 0.0), inverses[q]) for q in range(blocks)]
    inverses = [inverses[q] - dot3(inverses[q], mids[q]) for q in range(blocks)]
    for q in range(blocks):
        blocks_ref[q] = inverses[q]


def inverse_kernel(lower_ref, blocks_ref, th_ref, tl_ref, lh_ref, ll_ref, out_ref):
    total = lower_ref.shape[0]
    half = total // 2
    for start in range(0, total, 2 * BLOCK):
        at = start % half
        a, b = slice(start, start + BLOCK), slice(start + BLOCK, start + 2 * BLOCK)
        ac, bc = slice(at, at + BLOCK), slice(at + BLOCK, at + 2 * BLOCK)
        first, last = blocks_ref[start // BLOCK], blocks_ref[start // BLOCK + 1]
        out_ref[a, ac] = first
        out_ref[b, bc] = last
        out_ref[a, bc] = jnp.zeros((BLOCK, BLOCK), F32)
        out_ref[b, ac] = -dot3(last, dot3(lower_ref[b, a], first))
    quarter = half // 2
    for start in (0, half):
        a, b = slice(start, start + quarter), slice(start + quarter, start + half)
        out_ref[a, quarter:] = jnp.zeros((quarter, quarter), F32)
        out_ref[b, :quarter] = -dot3(out_ref[b, quarter:], dot3(lower_ref[b, a], out_ref[a, :quarter]))
    th_ref[...], tl_ref[...] = halves(out_ref[...])
    lh_ref[...], ll_ref[...] = halves(lower_ref[half:, :half])


def change_kernel(place_ref, order_ref, *refs):
    mine_ref, other_ref, th_ref, tl_ref, lh_ref, ll_ref, vec_ref, *held_refs, out_ref, sum_ref, w_ref, put_ref, put_sem = refs
    count, rows = vec_ref.shape
    core, x_at = place_ref[1], place_ref[2]
    for k in range(4):
        at = jnp.bitwise_xor(x_at, k) * 16
        sum_ref[span(core * 64 + at, 16), :] = mine_ref[k * 16 : k * 16 + 16, :]
        sum_ref[span((1 - core) * 64 + at, 16), :] = other_ref[k * 16 : k * 16 + 16, :]
    def times(x, high, low):
        xh, xl = halves(x)
        both = dot(jnp.concatenate([xh, xl], axis=0), high)
        return both[:count] + (both[count:] + dot(xh, low))

    half = sum_ref.shape[1] // 2
    order = order_ref[...]
    last = times(sum_ref[:, half:], th_ref[half:, :], tl_ref[half:, :])
    first = sum_ref[:, :half] - times(last, lh_ref[...], ll_ref[...])
    first = times(first, th_ref[:half, :], tl_ref[:half, :])
    for at, part in ((0, first), (half, last)):
        wh, wl = halves(part)
        w_ref[:count, at : at + half] = dot(order, wh).astype(BF16)
        w_ref[count:, at : at + half] = dot(order, wl).astype(BF16)

    copies = []
    edges = list(range(0, rows, WIDE)) + [rows - WIDE // 2, rows]
    for step, (at, end) in enumerate(zip(edges, edges[1:])):
        part = slice(at, end)
        split = held_refs[0].shape[0]
        high_ref, low_ref = held_refs[:2] if at < split else held_refs[2:]
        held = slice(at, end) if at < split else slice(at - split, end - split)
        both = dot(w_ref[...], high_ref[held, :], 1, 1)
        change = both[:count] + (both[count:] + dot(w_ref[:count, :], low_ref[held, :], 1, 1))
        put_ref[:, part] = vec_ref[:, part] - change
        copies.append(pltpu.make_async_copy(put_ref.at[:, part], out_ref.at[:, part], put_sem.at[step]))
        copies[-1].start()
    for copy in copies:
        copy.wait()


def params(mib):
    return pltpu.CompilerParams(vmem_limit_bytes=mib << 20)


def cost(flops, moved):
    return pl.CostEstimate(flops=flops, bytes_accessed=moved, transcendentals=0)


def swap(x, bits):
    return lax.ppermute(x, ("row", "col"), [(i, i ^ bits) for i in range(128)])


def gather(x, steps):
    across, far, near = (swap(x, bits) for bits in reversed(steps))
    return [x, near, across, far]


def small(kernel, shape, name, before, parts):
    after = [pl.BlockSpec(memory_space=pl.ANY)] * len(before)
    return pl.pallas_call(
        kernel,
        in_specs=after + [pl.BlockSpec(memory_space=pltpu.VMEM)] * len(parts),
        out_specs=pl.BlockSpec(memory_space=pltpu.VMEM),
        out_shape=jax.ShapeDtypeStruct(shape, F32),
        compiler_params=params(4),
        cost_estimate=cost(1 << 16, 1 << 16),
        name=name,
    )(*before, *parts)


def per_device(source_vectors, source_slot, reflectors, panel_offsets):
    row_count = lax.axis_size("row")
    col_count = lax.axis_size("col")
    src_block = source_vectors.shape[0]
    rows_dev, total = reflectors.shape
    width = total // panel_offsets.shape[0]
    count = src_block * row_count

    row = lax.axis_index("row")
    place = jnp.stack([row * rows_dev, row % 2, row // 4, lax.axis_index("col")]).astype(jnp.int32)
    lead = (panel_offsets[:, None] + jnp.arange(width, dtype=jnp.int32)[None, :]).reshape(1, total)
    placing = source_slot // (col_count * src_block) * src_block + source_slot % src_block
    order = (placing[:, None] == jnp.arange(count, dtype=jnp.int32)[None, :]).astype(BF16)

    smem = pl.BlockSpec(memory_space=pltpu.SMEM)
    vmem = pl.BlockSpec(memory_space=pltpu.VMEM)
    hbm = pl.BlockSpec(memory_space=pltpu.HBM)

    shaped = source_vectors.reshape(src_block, row_count, rows_dev).transpose(1, 0, 2)
    received = lax.all_to_all(shaped, "row", 0, 0, tiled=True).reshape(count, rows_dev)

    packed = 9 * BLOCK
    halved = pltpu.HBM((rows_dev, total), BF16)
    steps = rows_dev // WIDE
    high, low, keep, send = pl.pallas_call(
        gram_kernel,
        in_specs=[smem, vmem, hbm],
        out_specs=[hbm, hbm, vmem, vmem],
        out_shape=[halved, halved] + [jax.ShapeDtypeStruct((HALF, packed), F32)] * 2,
        scratch_shapes=[
            pltpu.VMEM((SLOTS, TILE, total), F32),
            pltpu.VMEM((2, TILE, total), BF16),
            pltpu.VMEM((2, TILE, total), BF16),
            pltpu.VMEM((2 * BLOCK, total), F32),
            pltpu.VMEM((2, HALF, packed), F32),
            pltpu.SemaphoreType.DMA((SLOTS,)),
            pltpu.SemaphoreType.DMA((2, 2)),
        ],
        compiler_params=params(20),
        cost_estimate=cost(12 * rows_dev * BLOCK * total, 8 * rows_dev * total),
        name="gram",
    )(place, lead, pltpu.with_memory_space_constraint(reflectors, pltpu.HBM))
    both = keep + swap(send, CORE)
    part = both[:16]
    for k, bits in ((1, 32), (3, 96), (2, 64)):
        part = part + swap(both[k * 16 : k * 16 + 16], bits)
    near = swap(part, Z_HIGH)

    after = pl.BlockSpec(memory_space=pl.ANY)
    high = pltpu.with_memory_space_constraint(high, pltpu.HBM)
    low = pltpu.with_memory_space_constraint(low, pltpu.HBM)
    split = (steps + 1) // 2 * WIDE
    first_held, last_held = ([pltpu.VMEM((n, total), BF16)] * 2 for n in (split, rows_dev - split))
    summed = jax.ShapeDtypeStruct((count, total), F32)
    semaphores = pltpu.SemaphoreType.DMA((steps, 2))
    first_high, first_low, sums = pl.pallas_call(
        first_product_kernel,
        in_specs=[after, vmem, hbm, hbm],
        out_specs=[vmem] * 3,
        out_shape=first_held + [summed],
        scratch_shapes=[semaphores],
        compiler_params=params(8),
        cost_estimate=cost(3 * rows_dev * count * total, 2 * rows_dev * total),
        name="product_first",
    )(part, received, high, low)
    piece = small(add_kernel, (16, packed), "gram_z", [sums], [part, near])
    pieces = gather(piece, X_STEPS)
    last_high, last_low, sums = pl.pallas_call(
        last_product_kernel,
        in_specs=[after, smem, vmem, vmem, hbm, hbm],
        out_specs=[vmem] * 3,
        out_shape=last_held + [summed],
        scratch_shapes=[pltpu.VMEM((count, total), F32), semaphores],
        compiler_params=params(8),
        cost_estimate=cost(3 * rows_dev * count * total, 2 * rows_dev * total),
        name="product_last",
    )(piece, place, sums, received, high, low)
    grams = small(join_kernel, (64, packed), "gram_x", [sums], pieces)
    pieces = gather(grams, Y_STEPS)
    send = small(split_kernel, (count // 2, total), "sum_split", [grams], [sums])
    ordered = pl.pallas_call(
        reorder_kernel,
        in_specs=[vmem, vmem],
        out_specs=vmem,
        out_shape=jax.ShapeDtypeStruct((count, rows_dev), F32),
        compiler_params=params(8),
        cost_estimate=cost(6 * rows_dev * count * count, 16 * rows_dev * count),
        name="reorder",
    )(order, received)
    both = small(add_kernel, (count // 2, total), "sum_core", [grams], [sums, swap(send, CORE)])
    parts = [both[: count // 8]]
    for k, bits in ((1, 32), (2, 64), (3, 96)):
        parts.append(swap(both[k * count // 8 : (k + 1) * count // 8], bits))
    sums = small(sum_kernel, (count // 8, total), "sum_x", [pieces[1]], parts)
    sums = small(add_kernel, (count // 8, total), "sum_z", [ordered], [sums, swap(sums, Z_HIGH)])
    before_y = sums
    sums = gather(sums, X_STEPS)
    grams = small(join_kernel, (256, packed), "gram_y", [before_y], pieces)
    lower, blocks = pl.pallas_call(
        blocks_kernel,
        in_specs=[smem] + [vmem] * 2,
        out_specs=[vmem] * 2,
        out_shape=[jax.ShapeDtypeStruct((total, total), F32), jax.ShapeDtypeStruct((total // BLOCK, BLOCK, BLOCK), F32)],
        scratch_shapes=[pltpu.VMEM((8, 64, packed), F32)],
        compiler_params=params(12),
        cost_estimate=cost(4 * total**3, 4 * total**2),
        name="inverse_blocks",
    )(place, grams, swap(grams, CORE))
    mine = small(join_kernel, (count // 2, total), "sum_join", [blocks], sums)
    other = swap(mine, CORE)
    inverses = pl.pallas_call(
        inverse_kernel,
        in_specs=[vmem] * 2,
        out_specs=[vmem] * 4,
        out_shape=[jax.ShapeDtypeStruct((total, total // 2), BF16)] * 2 + [jax.ShapeDtypeStruct((total // 2, total // 2), BF16)] * 2,
        scratch_shapes=[pltpu.VMEM((total, total // 2), F32)],
        compiler_params=params(12),
        cost_estimate=cost(4 * total**3, 4 * total**2),
        name="inverse",
    )(lower, blocks)

    return pl.pallas_call(
        change_kernel,
        in_specs=[smem] + [vmem] * 12,
        out_specs=hbm,
        out_shape=jax.ShapeDtypeStruct((count, rows_dev), F32),
        scratch_shapes=[
            pltpu.VMEM((count, total), F32),
            pltpu.VMEM((2 * count, total), BF16),
            pltpu.VMEM((count, rows_dev), F32),
            pltpu.SemaphoreType.DMA((steps + 1,)),
        ],
        compiler_params=params(12),
        cost_estimate=cost(6 * rows_dev * count * total, 4 * rows_dev * count),
        name="change",
    )(place, order, mine, other, *inverses, ordered, first_high, first_low, last_high, last_low)


def solution(mesh):
    in_specs = (P(("row", "col"), None), P("col"), P("row", None), P())
    out_specs = P("col", "row")
    return jax.shard_map(per_device, mesh=mesh, in_specs=in_specs, out_specs=out_specs, check_vma=False)
```

```python
import jax
import jax.numpy as jnp
from jax import lax
from jax.experimental import pallas as pl
from jax.experimental.pallas import tpu as pltpu
from jax.sharding import PartitionSpec as P

F32 = jnp.float32
BF16 = jnp.bfloat16
TILE = 256
WIDE = 512
CHUNK = 16
SLOTS = 4
BLOCK = 128
HALF = 64
CORE, Z_HIGH, Z_LOW = 8, 16, 4
X_STEPS = (32, 96, 64)
Y_STEPS = (1, 3, 2)


def halves(x):
    high = x.astype(BF16)
    return high, (x - high.astype(F32)).astype(BF16)


def dot(a, b, ca=1, cb=0):
    return lax.dot_general(a, b, (((ca,), (cb,)), ((), ())), preferred_element_type=F32)


def dot3(a, b):
    m, n = a.shape[0], b.shape[1]
    both = dot(jnp.concatenate(halves(a), axis=0), jnp.concatenate(halves(b), axis=1))
    return both[:m, :n] + (both[:m, n:] + both[m:, :n])


def span(start, size):
    return pl.ds(start if isinstance(start, int) else pl.multiple_of(start, size), size)


def sweep(first, lead_ref, tiles_ref, slot_ref, even_ref, odd_ref, sem, put_sem, prepare, use, high_ref, low_ref):
    steps = tiles_ref.shape[0] // TILE
    total = tiles_ref.shape[1]
    index = lax.broadcasted_iota(jnp.int32, (CHUNK, total), 0)

    def fetch(step):
        slot = step % SLOTS if isinstance(step, int) else lax.rem(step, SLOTS)
        return pltpu.make_async_copy(tiles_ref.at[span(step * TILE, TILE), :], slot_ref.at[slot], sem.at[slot])

    def put(step, ref, at):
        part = span(step * TILE, TILE)
        return (
            pltpu.make_async_copy(ref.at[0], high_ref.at[part, :], put_sem.at[at, 0]),
            pltpu.make_async_copy(ref.at[1], low_ref.at[part, :], put_sem.at[at, 1]),
        )

    def halve(step, ref, quarter):
        slot = step % SLOTS if isinstance(step, int) else lax.rem(step, SLOTS)
        start = lead_ref[...] - (first + step * TILE)
        for at in range(quarter * TILE // 4, (quarter + 1) * TILE // 4, CHUNK):
            x = slot_ref[slot, at : at + CHUNK, :]
            lead = start - at
            x = jnp.where(index < lead, 0.0, jnp.where(index == lead, 1.0, x))
            high, low = halves(x)
            ref[0, at : at + CHUNK, :] = high
            ref[1, at : at + CHUNK, :] = low

    def work(step, now, later):
        left = prepare(step, now)
        for quarter in range(4):
            use(left, now, quarter)
            if later is not None:
                halve(step + 1, later, quarter)

    for step in range(SLOTS - 1):
        fetch(step).start()
    fetch(0).wait()
    for quarter in range(4):
        halve(0, even_ref, quarter)
    for copy in put(0, even_ref, 0):
        copy.start()

    @pl.loop(0, steps // 2 - 1)
    def _(pair):
        for step, now, later, at in ((2 * pair, even_ref, odd_ref, 1), (2 * pair + 1, odd_ref, even_ref, 0)):

            @pl.when(step + SLOTS - 1 < steps)
            def _():
                fetch(step + SLOTS - 1).start()

            @pl.when(step >= 1)
            def _():
                for copy in put(step - 1, later, at):
                    copy.wait()

            fetch(step + 1).wait()
            work(step, now, later)
            for copy in put(step + 1, later, at):
                copy.start()

    fetch(steps - 1).wait()
    for copy in put(steps - 3, odd_ref, 1):
        copy.wait()
    work(steps - 2, even_ref, odd_ref)
    for copy in put(steps - 1, odd_ref, 1):
        copy.start()
    work(steps - 1, odd_ref, None)
    for copy in put(steps - 2, even_ref, 0) + put(steps - 1, odd_ref, 1):
        copy.wait()


def add_product(sum_ref):
    count, total = sum_ref.shape
    part = total // 4

    def use(left, ref, quarter):
        at = slice(quarter * part, (quarter + 1) * part)
        both = dot(left, ref[0, :, at])
        sum_ref[:, at] += both[:count] + (both[count:] + dot(left[:count], ref[1, :, at]))

    return use


def gram_kernel(
    place_ref, lead_ref, tiles_ref, high_ref, low_ref, keep_ref, send_ref, slot_ref, even_ref, odd_ref, sum_ref, pack_ref, sem, put_sem
):
    total = tiles_ref.shape[1]
    first, core, x_at, col = place_ref[0], place_ref[1], place_ref[2], place_ref[3]
    lane_half = lax.broadcasted_iota(jnp.int32, (1, BLOCK), 1) // HALF
    turns = []
    for turn in (lax.rem(col, 4), 7 - lax.rem(col, 4)):
        parity = lax.rem(turn, 2)
        from_a = jnp.where(lane_half == parity, 1.0, 0.0).astype(BF16)
        from_b = jnp.where(lane_half == parity, 0.0, 1.0).astype(BF16)
        turns.append((parity, turn // 2, (15 - turn) // 2, from_a, from_b))

    def prepare(step, ref):
        def chosen(which, block_a, block_b, from_a, from_b):
            a = ref[which, :, span(block_a * BLOCK, BLOCK)]
            b = ref[which, :, span(block_b * BLOCK, BLOCK)]
            return a * from_a + b * from_b

        return jnp.concatenate([chosen(which, *turn[1:]) for which in (0, 1) for turn in turns], axis=1).T

    sum_ref[...] = jnp.zeros_like(sum_ref)
    sweep(
        first, lead_ref, tiles_ref, slot_ref, even_ref, odd_ref, sem, put_sem, prepare, add_product(sum_ref), high_ref, low_ref
    )

    for p, (parity, block_a, block_b, _, _) in enumerate(turns):
        pack_ref[p, :, :total] = sum_ref[span(p * BLOCK + (1 - parity) * HALF, HALF), :]
        for m in range(4):

            @pl.when(m <= block_a)
            def _():
                pack_ref[p, :, span((block_b + 1 + m) * BLOCK, BLOCK)] = sum_ref[
                    span(p * BLOCK + parity * HALF, HALF), m * BLOCK : (m + 1) * BLOCK
                ]

        for k in range(4):
            at = jnp.bitwise_xor(x_at, k) * 8
            to = slice(k * 16 + p * 8, k * 16 + p * 8 + 8)
            keep_ref[to, :] = pack_ref[p, span(core * 32 + at, 8), :]
            send_ref[to, :] = pack_ref[p, span((1 - core) * 32 + at, 8), :]


def product_copies(from_refs, to_refs, first, sem):
    rows = to_refs[0].shape[0]
    return [
        [
            pltpu.make_async_copy(a.at[first + at : first + at + WIDE, :], b.at[at : at + WIDE, :], sem.at[at // WIDE, i])
            for i, (a, b) in enumerate(zip(from_refs, to_refs))
        ]
        for at in range(0, rows, WIDE)
    ]


def product(vec_ref, from_refs, to_refs, first, sem, sum_ref, total):
    copies = product_copies(from_refs, to_refs, first, sem)
    count = vec_ref.shape[0]
    for pair in copies:
        for copy in pair:
            copy.start()
    for step, pair in enumerate(copies):
        at = step * WIDE
        left = jnp.concatenate(halves(vec_ref[:, first + at : first + at + WIDE]), axis=0)
        for copy in pair:
            copy.wait()
        both = dot(left, to_refs[0][at : at + WIDE, :])
        added = both[:count] + (both[count:] + dot(left[:count], to_refs[1][at : at + WIDE, :]))
        if total is not None:
            added = added + total[...]
        total = sum_ref
        sum_ref[...] = added


def first_product_kernel(_, vec_ref, from_high_ref, from_low_ref, high_ref, low_ref, sum_ref, sem):
    product(vec_ref, (from_high_ref, from_low_ref), (high_ref, low_ref), 0, sem, sum_ref, None)


def last_product_kernel(
    _, place_ref, total_ref, vec_ref, from_high_ref, from_low_ref, high_ref, low_ref, out_ref, sum_ref, sem
):
    first = vec_ref.shape[1] - high_ref.shape[0]
    product(vec_ref, (from_high_ref, from_low_ref), (high_ref, low_ref), first, sem, sum_ref, total_ref)
    core, x_at = place_ref[1], place_ref[2]
    for k in range(8):
        at = jnp.bitwise_xor(core, k // 4) * 64 + jnp.bitwise_xor(x_at, k % 4) * 16
        out_ref[k * 16 : k * 16 + 16, :] = sum_ref[span(at, 16), :]


def split_kernel(_, sum_ref, send_ref):
    send_ref[...] = sum_ref[send_ref.shape[0] :, :]


def add_kernel(*refs):
    *_, a_ref, b_ref, out_ref = refs
    out_ref[...] = a_ref[: b_ref.shape[0], :] + b_ref[...]


def join_kernel(_, *refs):
    *parts, out_ref = refs
    at = 0
    for part in parts:
        out_ref[at : at + part.shape[0], :] = part[...]
        at += part.shape[0]


def sum_kernel(_, *refs):
    *parts, out_ref = refs
    a, b, c, d = (part[...] for part in parts)
    out_ref[...] = (a + b) + (c + d)


def reorder_kernel(order_ref, vec_ref, out_ref):
    order = order_ref[...]

    @pl.loop(0, vec_ref.shape[1] // WIDE)
    def _(step):
        part = span(step * WIDE, WIDE)
        value = vec_ref[:, part]
        v1 = value.astype(BF16)
        rest = value - v1.astype(F32)
        v2, v3 = halves(rest)
        out_ref[:, part] = dot(order, v1) + (dot(order, v2) + dot(order, v3))


def blocks_kernel(place_ref, *refs):
    *gram_refs, lower_ref, blocks_ref, stage_ref = refs
    total = lower_ref.shape[0]
    blocks = total // BLOCK
    core, x_at, col = place_ref[1], place_ref[2], place_ref[3]
    r = lax.broadcasted_iota(jnp.int32, (BLOCK, BLOCK), 0)
    c = lax.broadcasted_iota(jnp.int32, (BLOCK, BLOCK), 1)
    for j in range(8):
        to = jnp.bitwise_xor(core, j // 4) * 4 + jnp.bitwise_xor(lax.rem(col, 4), j % 4)
        stage_ref[to] = gram_refs[j // 4][j % 4 * 64 : j % 4 * 64 + 64, :]
    for q in range(8):
        width = (q // 2 + 1) * BLOCK
        rest = 9 * BLOCK - width
        for k in range(8):
            at = jnp.bitwise_xor(x_at, k % 4) * 16 + q // 4 * 8
            piece = stage_ref[k // 4 * 4 + (q if q < 4 else 7 - q), span(at, 8), :]
            top, low = (15 - q) * HALF + k * 8, q * HALF + k * 8
            lower_ref[top : top + 8, :rest] = piece[:, :rest]
            lower_ref[low : low + 8, :width] = piece[:, rest:]
    lows, inverses = [], []
    for q in range(blocks):
        part = pl.ds(q * BLOCK, BLOCK)
        square = lower_ref[part, part]
        lows.append(square)
        inverses.append(jnp.where(r == c, 2.0 / square, 0.0))
    same = r // HALF == c // HALF
    scales = [jnp.sum(inverses[q], axis=0, keepdims=True) for q in range(blocks)]
    scaled = [jnp.sum(inverses[q], axis=1, keepdims=True) for q in range(blocks)]
    powers = [jnp.where(same & (r > c), -lows[q] * scaled[q], 0.0) for q in range(blocks)]
    identity = jnp.where(r == c, 1.0, 0.0)
    products = [identity + powers[q] for q in range(blocks)]
    powers = [dot3(power, power) for power in powers]
    for _ in range(4):
        both = [dot3(jnp.concatenate([powers[q], products[q]], axis=0), powers[q]) for q in range(blocks)]
        powers = [part[:BLOCK] for part in both]
        products = [products[q] + both[q][BLOCK:] for q in range(blocks)]
    products = [products[q] + dot3(products[q], powers[q]) for q in range(blocks)]
    inverses = [products[q] * scales[q] for q in range(blocks)]
    pair = (r >= HALF) & (c < HALF)
    mids = [dot3(jnp.where(pair, lows[q], 0.0), inverses[q]) for q in range(blocks)]
    inverses = [inverses[q] - dot3(inverses[q], mids[q]) for q in range(blocks)]
    for q in range(blocks):
        blocks_ref[q] = inverses[q]


def inverse_kernel(lower_ref, blocks_ref, th_ref, tl_ref, lh_ref, ll_ref, out_ref):
    total = lower_ref.shape[0]
    half = total // 2
    for start in range(0, total, 2 * BLOCK):
        at = start % half
        a, b = slice(start, start + BLOCK), slice(start + BLOCK, start + 2 * BLOCK)
        ac, bc = slice(at, at + BLOCK), slice(at + BLOCK, at + 2 * BLOCK)
        first, last = blocks_ref[start // BLOCK], blocks_ref[start // BLOCK + 1]
        out_ref[a, ac] = first
        out_ref[b, bc] = last
        out_ref[a, bc] = jnp.zeros((BLOCK, BLOCK), F32)
        out_ref[b, ac] = -dot3(last, dot3(lower_ref[b, a], first))
    quarter = half // 2
    for start in (0, half):
        a, b = slice(start, start + quarter), slice(start + quarter, start + half)
        out_ref[a, quarter:] = jnp.zeros((quarter, quarter), F32)
        out_ref[b, :quarter] = -dot3(out_ref[b, quarter:], dot3(lower_ref[b, a], out_ref[a, :quarter]))
    th_ref[...], tl_ref[...] = halves(out_ref[...])
    lh_ref[...], ll_ref[...] = halves(lower_ref[half:, :half])


def change_kernel(place_ref, order_ref, *refs):
    mine_ref, other_ref, th_ref, tl_ref, lh_ref, ll_ref, vec_ref, *held_refs, out_ref, sum_ref, w_ref, put_ref, put_sem = refs
    count, rows = vec_ref.shape
    core, x_at = place_ref[1], place_ref[2]
    for k in range(4):
        at = jnp.bitwise_xor(x_at, k) * 16
        sum_ref[span(core * 64 + at, 16), :] = mine_ref[k * 16 : k * 16 + 16, :]
        sum_ref[span((1 - core) * 64 + at, 16), :] = other_ref[k * 16 : k * 16 + 16, :]
    def times(x, high, low):
        xh, xl = halves(x)
        both = dot(jnp.concatenate([xh, xl], axis=0), high)
        return both[:count] + (both[count:] + dot(xh, low))

    half = sum_ref.shape[1] // 2
    order = order_ref[...]
    last = times(sum_ref[:, half:], th_ref[half:, :], tl_ref[half:, :])
    first = sum_ref[:, :half] - times(last, lh_ref[...], ll_ref[...])
    first = times(first, th_ref[:half, :], tl_ref[:half, :])
    for at, part in ((0, first), (half, last)):
        wh, wl = halves(part)
        w_ref[:count, at : at + half] = dot(order, wh).astype(BF16)
        w_ref[count:, at : at + half] = dot(order, wl).astype(BF16)

    copies = []
    edges = list(range(0, rows, WIDE)) + [rows - WIDE // 2, rows]
    for step, (at, end) in enumerate(zip(edges, edges[1:])):
        part = slice(at, end)
        split = held_refs[0].shape[0]
        high_ref, low_ref = held_refs[:2] if at < split else held_refs[2:]
        held = slice(at, end) if at < split else slice(at - split, end - split)
        both = dot(w_ref[...], high_ref[held, :], 1, 1)
        change = both[:count] + (both[count:] + dot(w_ref[:count, :], low_ref[held, :], 1, 1))
        put_ref[:, part] = vec_ref[:, part] - change
        copies.append(pltpu.make_async_copy(put_ref.at[:, part], out_ref.at[:, part], put_sem.at[step]))
        copies[-1].start()
    for copy in copies:
        copy.wait()


def params(mib):
    return pltpu.CompilerParams(vmem_limit_bytes=mib << 20)


def cost(flops, moved):
    return pl.CostEstimate(flops=flops, bytes_accessed=moved, transcendentals=0)


def swap(x, bits):
    return lax.ppermute(x, ("row", "col"), [(i, i ^ bits) for i in range(128)])


def gather(x, steps):
    across, far, near = (swap(x, bits) for bits in reversed(steps))
    return [x, near, across, far]


def small(kernel, shape, name, before, parts):
    after = [pl.BlockSpec(memory_space=pl.ANY)] * len(before)
    return pl.pallas_call(
        kernel,
        in_specs=after + [pl.BlockSpec(memory_space=pltpu.VMEM)] * len(parts),
        out_specs=pl.BlockSpec(memory_space=pltpu.VMEM),
        out_shape=jax.ShapeDtypeStruct(shape, F32),
        compiler_params=params(4),
        cost_estimate=cost(1 << 16, 1 << 16),
        name=name,
    )(*before, *parts)


def per_device(source_vectors, source_slot, reflectors, panel_offsets):
    row_count = lax.axis_size("row")
    col_count = lax.axis_size("col")
    src_block = source_vectors.shape[0]
    rows_dev, total = reflectors.shape
    width = total // panel_offsets.shape[0]
    count = src_block * row_count

    row = lax.axis_index("row")
    place = jnp.stack([row * rows_dev, row % 2, row // 4, lax.axis_index("col")]).astype(jnp.int32)
    lead = (panel_offsets[:, None] + jnp.arange(width, dtype=jnp.int32)[None, :]).reshape(1, total)
    placing = source_slot // (col_count * src_block) * src_block + source_slot % src_block
    order = (placing[:, None] == jnp.arange(count, dtype=jnp.int32)[None, :]).astype(BF16)

    smem = pl.BlockSpec(memory_space=pltpu.SMEM)
    vmem = pl.BlockSpec(memory_space=pltpu.VMEM)
    hbm = pl.BlockSpec(memory_space=pltpu.HBM)

    shaped = source_vectors.reshape(src_block, row_count, rows_dev).transpose(1, 0, 2)
    received = lax.all_to_all(shaped, "row", 0, 0, tiled=True).reshape(count, rows_dev)

    packed = 9 * BLOCK
    halved = pltpu.HBM((rows_dev, total), BF16)
    steps = rows_dev // WIDE
    high, low, keep, send = pl.pallas_call(
        gram_kernel,
        in_specs=[smem, vmem, hbm],
        out_specs=[hbm, hbm, vmem, vmem],
        out_shape=[halved, halved] + [jax.ShapeDtypeStruct((HALF, packed), F32)] * 2,
        scratch_shapes=[
            pltpu.VMEM((SLOTS, TILE, total), F32),
            pltpu.VMEM((2, TILE, total), BF16),
            pltpu.VMEM((2, TILE, total), BF16),
            pltpu.VMEM((2 * BLOCK, total), F32),
            pltpu.VMEM((2, HALF, packed), F32),
            pltpu.SemaphoreType.DMA((SLOTS,)),
            pltpu.SemaphoreType.DMA((2, 2)),
        ],
        compiler_params=params(20),
        cost_estimate=cost(12 * rows_dev * BLOCK * total, 8 * rows_dev * total),
        name="gram",
    )(place, lead, pltpu.with_memory_space_constraint(reflectors, pltpu.HBM))
    both = keep + swap(send, CORE)
    part = both[:16]
    for k, bits in ((2, 64), (3, 96), (1, 32)):
        part = part + swap(both[k * 16 : k * 16 + 16], bits)
    near = swap(part, Z_HIGH)

    after = pl.BlockSpec(memory_space=pl.ANY)
    high = pltpu.with_memory_space_constraint(high, pltpu.HBM)
    low = pltpu.with_memory_space_constraint(low, pltpu.HBM)
    split = (steps + 1) // 2 * WIDE
    first_held, last_held = ([pltpu.VMEM((n, total), BF16)] * 2 for n in (split, rows_dev - split))
    summed = jax.ShapeDtypeStruct((count, total), F32)
    semaphores = pltpu.SemaphoreType.DMA((steps, 2))
    first_high, first_low, sums = pl.pallas_call(
        first_product_kernel,
        in_specs=[after, vmem, hbm, hbm],
        out_specs=[vmem] * 3,
        out_shape=first_held + [summed],
        scratch_shapes=[semaphores],
        compiler_params=params(8),
        cost_estimate=cost(3 * rows_dev * count * total, 2 * rows_dev * total),
        name="product_first",
    )(part, received, high, low)
    piece = small(add_kernel, (16, packed), "gram_z", [sums], [part, near])
    pieces = gather(piece, X_STEPS)
    last_high, last_low, sums = pl.pallas_call(
        last_product_kernel,
        in_specs=[after, smem, vmem, vmem, hbm, hbm],
        out_specs=[vmem] * 3,
        out_shape=last_held + [summed],
        scratch_shapes=[pltpu.VMEM((count, total), F32), semaphores],
        compiler_params=params(8),
        cost_estimate=cost(3 * rows_dev * count * total, 2 * rows_dev * total),
        name="product_last",
    )(piece, place, sums, received, high, low)
    grams = small(join_kernel, (64, packed), "gram_x", [sums], pieces)
    pieces = gather(grams, Y_STEPS)
    send = small(split_kernel, (count // 2, total), "sum_split", [grams], [sums])
    ordered = pl.pallas_call(
        reorder_kernel,
        in_specs=[vmem, vmem],
        out_specs=vmem,
        out_shape=jax.ShapeDtypeStruct((count, rows_dev), F32),
        compiler_params=params(8),
        cost_estimate=cost(6 * rows_dev * count * count, 16 * rows_dev * count),
        name="reorder",
    )(order, received)
    both = small(add_kernel, (count // 2, total), "sum_core", [grams], [sums, swap(send, CORE)])
    parts = [both[: count // 8]]
    for k, bits in ((1, 32), (2, 64), (3, 96)):
        parts.append(swap(both[k * count // 8 : (k + 1) * count // 8], bits))
    sums = small(sum_kernel, (count // 8, total), "sum_x", [pieces[1]], parts)
    sums = small(add_kernel, (count // 8, total), "sum_z", [ordered], [sums, swap(sums, Z_HIGH)])
    before_y = sums
    sums = gather(sums, X_STEPS)
    grams = small(join_kernel, (256, packed), "gram_y", [before_y], pieces)
    lower, blocks = pl.pallas_call(
        blocks_kernel,
        in_specs=[smem] + [vmem] * 2,
        out_specs=[vmem] * 2,
        out_shape=[jax.ShapeDtypeStruct((total, total), F32), jax.ShapeDtypeStruct((total // BLOCK, BLOCK, BLOCK), F32)],
        scratch_shapes=[pltpu.VMEM((8, 64, packed), F32)],
        compiler_params=params(12),
        cost_estimate=cost(4 * total**3, 4 * total**2),
        name="inverse_blocks",
    )(place, grams, swap(grams, CORE))
    mine = small(join_kernel, (count // 2, total), "sum_join", [blocks], sums)
    other = swap(mine, CORE)
    inverses = pl.pallas_call(
        inverse_kernel,
        in_specs=[vmem] * 2,
        out_specs=[vmem] * 4,
        out_shape=[jax.ShapeDtypeStruct((total, total // 2), BF16)] * 2 + [jax.ShapeDtypeStruct((total // 2, total // 2), BF16)] * 2,
        scratch_shapes=[pltpu.VMEM((total, total // 2), F32)],
        compiler_params=params(12),
        cost_estimate=cost(4 * total**3, 4 * total**2),
        name="inverse",
    )(lower, blocks)

    return pl.pallas_call(
        change_kernel,
        in_specs=[smem] + [vmem] * 12,
        out_specs=hbm,
        out_shape=jax.ShapeDtypeStruct((count, rows_dev), F32),
        scratch_shapes=[
            pltpu.VMEM((count, total), F32),
            pltpu.VMEM((2 * count, total), BF16),
            pltpu.VMEM((count, rows_dev), F32),
            pltpu.SemaphoreType.DMA((steps + 1,)),
        ],
        compiler_params=params(12),
        cost_estimate=cost(6 * rows_dev * count * total, 4 * rows_dev * count),
        name="change",
    )(place, order, mine, other, *inverses, ordered, first_high, first_low, last_high, last_low)


def solution(mesh):
    in_specs = (P(("row", "col"), None), P("col"), P("row", None), P())
    out_specs = P("col", "row")
    return jax.shard_map(per_device, mesh=mesh, in_specs=in_specs, out_specs=out_specs, check_vma=False)
```
